512 devices in a mesh: row: 16 (over z, core), col: 32 (over y, x).
Axes of the slice: x: 4, y: 8, z: 8, core: 2. Of those that a mesh axis runs over, the one named last changes fastest.
Arguments:
- query_tokens: bfloat16 [512, 32, 128], P('row'), may hold values from -14 to 14
- query_lengths: int32 [512], P('row'), may hold values from 8 to 32
- passage_tokens: bfloat16 [4096, 176, 128], P(('col', 'row')), may hold values from -8 to 8
- passage_lengths: int32 [4096], P(('col', 'row')), may hold values from 44 to 176
- student_queries: bfloat16 [512, 768], P('row', 'col'), may hold values from -28 to 28
- student_passages: bfloat16 [4096, 768], P('col', 'row'), may hold values from -0.21875 to 0.21875
- positives: int32 [512], P('row'), may hold values from 0 to 4095
Outputs:
- query_grads: float32 [512, 768], P('row', 'col')
- passage_grads: float32 [4096, 768], P('col', 'row')
- loss: float32 [], replicated
The draws below stay inside these ranges and needn't reach their ends.
All inputs are finite; a program needn't handle non-finite values.
Results may differ from the reference program's by a relative error of at most 0.00045.
Values may be sent and summed in bfloat16 or wider, within the bound.
A program may use at most 64 MiB of HBM per device.

```python
import math
import jax
import jax.numpy as jnp
from jax import lax

LQ = 32
LP = 176
E = 128
DS = 768
Q = 512
P_SIZE = 4096


def token_base(key, scale_span):
    normal_key = jax.random.fold_in(key, 0)
    scale_key = jax.random.fold_in(key, 2)
    normal_values = jnp.clip(jax.random.normal(normal_key, (Q, LQ, E), jnp.float32), -6.0, 6.0)
    values = normal_values
    scales = jnp.exp(jax.random.uniform(scale_key, (Q, 1, 1), jnp.float32, 0.0, math.log(scale_span)))
    return (values, scales)


def draw_query_tokens(key, part):
    values, scales = token_base(key, 1.0)
    return (values * scales).astype(jnp.bfloat16)


def draw_passage_tokens(key, part):
    values, scales = token_base(key, 1.0)
    low_level = 0.8
    high_level = 1.25
    key = jax.random.fold_in(key, 37)
    noise_key, level_key, owner_key, source_key, target_key, strength_key = jax.random.split(key, 6)
    background = jnp.clip(jax.random.normal(noise_key, (P_SIZE, LP, E), jnp.float32), -6.0, 6.0) / math.sqrt(E)
    levels = jnp.exp(jax.random.uniform(level_key, (P_SIZE, 1, 1), jnp.float32, math.log(low_level), math.log(high_level)))
    owner_query = jax.random.randint(owner_key, (P_SIZE,), 0, Q)
    owner_slot = jax.random.randint(source_key, (P_SIZE,), 0, max(LQ // 4, 1))
    passage_slot = jax.random.randint(target_key, (P_SIZE,), 0, max(LP // 4, 1))
    strength = jnp.exp(jax.random.uniform(strength_key, (P_SIZE, 1), jnp.float32, math.log(1.5), math.log(5.0)))
    planted = values[owner_query, owner_slot] * strength / math.sqrt(E)
    planted_slot = (jnp.arange(LP)[None, :] == passage_slot[:, None])[:, :, None]
    tokens = jnp.where(planted_slot, planted[:, None, :], background * levels)
    return tokens.astype(jnp.bfloat16)


def draw_student_queries(key, part):
    key = jax.random.fold_in(key, 23)
    values = jax.random.normal(key, (Q, DS), jnp.float32)
    return jnp.clip(values, -6.0, 6.0).astype(jnp.bfloat16)


def touch_ends(values, rng, low, high):
    extent = values.shape
    place = [jax.random.randint(jax.random.fold_in(rng, axis), (), 0, extent[axis]) for axis in range(len(extent))]
    values = values.at[tuple(place)].set(low)
    longest = extent.index(max(extent))
    place[longest] = (place[longest] + 1) % extent[longest]
    return values.at[tuple(place)].set(high)


def block_scale(own_key, extent, shards, least, high):
    def one(axis_at, shards_of):
        heights = jax.random.uniform(jax.random.fold_in(jax.random.fold_in(own_key, 6), axis_at), (shards_of,), jnp.float32, least / len(shards), high / len(shards))
        return jnp.repeat(jnp.exp(heights), extent[axis_at] // shards_of).reshape((-1,) + (1,) * (len(extent) - axis_at - 1))

    factor_of = one(*shards[0])
    for cut in shards[1:]:
        factor_of = factor_of * one(*cut)
    return factor_of


def noise(key, dims, width, reach, cuts=(), kind=jnp.bfloat16):
    drawn = width * jax.random.normal(key, dims, jnp.float32)
    if cuts:
        drawn = drawn * block_scale(key, dims, cuts, -0.22, 0.18)
    return jnp.clip(drawn, -reach, reach).astype(kind)


def setup_inputs(seed: int = 0) -> dict:
    arg_keys = jax.random.split(jax.random.key(seed), 8)
    query_tokens = draw_query_tokens(jax.random.fold_in(arg_keys[7], 71), 0)
    query_lengths = touch_ends(jax.random.randint(arg_keys[1], (Q,), max(LQ // 4, 1), LQ + 1), jax.random.fold_in(arg_keys[1], 1), max(LQ // 4, 1), LQ).astype(jnp.int32)
    passage_tokens = draw_passage_tokens(jax.random.fold_in(arg_keys[7], 71), 0)
    passage_lengths = touch_ends(jax.random.randint(arg_keys[3], (P_SIZE,), max(LP // 4, 1), LP + 1), jax.random.fold_in(arg_keys[3], 1), max(LP // 4, 1), LP).astype(jnp.int32)
    student_queries = draw_student_queries(jax.random.fold_in(arg_keys[7], 71), 0)
    student_passages = noise(arg_keys[5], (P_SIZE, DS), DS ** -0.5, 0.21875, ((0, 32), (1, 16)))
    positives = touch_ends(jax.random.randint(arg_keys[6], (Q,), 0, P_SIZE), jax.random.fold_in(arg_keys[6], 1), 0, P_SIZE - 1).astype(jnp.int32)
    return {"query_tokens": query_tokens, "query_lengths": query_lengths, "passage_tokens": passage_tokens, "passage_lengths": passage_lengths, "student_queries": student_queries, "student_passages": student_passages, "positives": positives}


NEG = -1e30
SCALE = 4.0


def reference(query_tokens, query_lengths, passage_tokens, passage_lengths, student_queries, student_passages, positives):
    query_mask = (jnp.arange(LQ)[None, :] < query_lengths[:, None]).astype(jnp.float32)
    passage_valid = jnp.arange(LP)[None, :] < passage_lengths[:, None]
    passage_flat = passage_tokens.astype(jnp.float32).reshape(P_SIZE * LP, E)
    blocks = query_tokens.astype(jnp.float32).reshape(Q // 4, 4 * LQ, E)
    masks = query_mask.reshape(Q // 4, 4, LQ)

    def one_block(items):
        block, mask_rows = items
        sims = jnp.dot(block, passage_flat.T, precision=lax.Precision.HIGHEST).reshape(4 * LQ, P_SIZE, LP)
        sims = jnp.where(passage_valid[None], sims, NEG)
        maxima = jnp.max(sims, axis=2).reshape(4, LQ, P_SIZE)
        return jnp.sum(maxima * mask_rows[:, :, None], axis=1)

    teacher = lax.map(one_block, (blocks, masks)).reshape(Q, P_SIZE)
    student = SCALE * jnp.dot(student_queries, student_passages.T, preferred_element_type=jnp.float32)
    teacher_max = jnp.max(teacher, axis=1, keepdims=True)
    student_max = jnp.max(student, axis=1, keepdims=True)
    teacher_exp = jnp.exp(teacher - teacher_max)
    student_exp = jnp.exp(student - student_max)
    teacher_sum = jnp.sum(teacher_exp, axis=1, keepdims=True)
    student_sum = jnp.sum(student_exp, axis=1, keepdims=True)
    cross = jnp.sum(teacher_exp * (teacher - student), axis=1, keepdims=True)
    onehot = (jnp.arange(P_SIZE)[None, :] == positives[:, None])
    positive_score = jnp.sum(jnp.where(onehot, student, 0.0), axis=1, keepdims=True)
    teacher_lse = teacher_max + jnp.log(teacher_sum)
    student_lse = student_max + jnp.log(student_sum)
    per_query = cross / teacher_sum - teacher_lse + 2.0 * student_lse - positive_score
    loss = jnp.sum(per_query) / Q
    teacher_probs = teacher_exp / teacher_sum
    student_probs = student_exp / student_sum
    slope = (2.0 * student_probs - teacher_probs - onehot.astype(jnp.float32)) / Q
    query_grads = SCALE * jnp.dot(slope, student_passages.astype(jnp.float32), precision=lax.Precision.HIGHEST)
    passage_grads = SCALE * jnp.dot(slope.T, student_queries.astype(jnp.float32), precision=lax.Precision.HIGHEST)
    return query_grads, passage_grads, loss
```

```python
import functools

import jax
import jax.numpy as jnp
from jax import lax
from jax.experimental import pallas as pl
from jax.experimental.pallas import tpu as pltpu
from jax.sharding import PartitionSpec as P

MESH = pl.DeviceIdType.MESH
SCALE = 4.0
X_CHIPS = 4
QB = 32
GROUPS = 128 // QB
BF = jnp.bfloat16
F32 = jnp.float32


def nt(a, b):
    return lax.dot_general(a, b, (((1,), (1,)), ((), ())), preferred_element_type=F32)


def nn(a, b):
    return lax.dot_general(a, b, (((1,), (0,)), ((), ())), preferred_element_type=F32)


def split2(v):
    hi = v.astype(BF)
    return hi, (v - hi.astype(F32)).astype(BF)


def spread(v):
    v = v + pltpu.roll(v, 64, 1)
    return v + pltpu.roll(v, 32, 1)


def kernel(
    R,
    C,
    qt_ref,
    qlen_ref,
    pt_ref,
    plen_ref,
    sq_ref,
    sp_ref,
    pos_ref,
    pg_ref,
    qg_ref,
    loss_ref,
    qraw,
    praw,
    qbuf,
    xbuf,
    sqx,
    spt,
    sst,
    sbuf,
    upz,
    vbuf,
    zag,
    zfull,
    sqr,
    tblk,
    town,
    tag,
    upt,
    ubuf,
    fin,
    in_sem,
    z_send,
    z_recv,
    xy_send,
    xy_recv,
    sib_send,
    sib_recv,
    many_send,
    many_recv,
):
    Z = R // 2
    XC = min(X_CHIPS, C)
    YC = C // XC
    L = qt_ref.shape[1]
    LP = pt_ref.shape[1]
    N = QB * L
    SL = N // 4
    HALF = SL // 2
    PB = 8 * R
    PR = C // R
    DR = 24 * PR
    T = R // GROUPS
    total = QB * R

    r = lax.axis_index("row")
    c = lax.axis_index("col")
    z = lax.div(r, 2)
    k = lax.rem(r, 2)
    x = lax.rem(c, XC)
    y = lax.div(c, XC)
    color = lax.rem(x + 2 * y, 4)

    def row_of(zz, kk):
        return lax.rem(zz + 2 * Z, Z) * 2 + kk

    def col_of(xx, yy):
        return lax.rem(yy + YC, YC) * XC + lax.rem(xx + XC, XC)

    def send(src, dst, s_sem, r_sem, **where):
        pltpu.make_async_remote_copy(
            src_ref=src, dst_ref=dst, send_sem=s_sem, recv_sem=r_sem, device_id=where, device_id_type=MESH
        ).start()

    def got(dst, r_sem):
        pltpu.make_async_remote_copy(
            src_ref=dst, dst_ref=dst, send_sem=r_sem, recv_sem=r_sem, device_id={"row": r}, device_id_type=MESH
        ).wait_recv()

    def left(src, s_sem):
        pltpu.make_async_remote_copy(
            src_ref=src, dst_ref=src, send_sem=s_sem, recv_sem=s_sem, device_id={"row": r}, device_id_type=MESH
        ).wait_send()

    q_in = pltpu.make_async_copy(qt_ref, qraw, in_sem.at[0])
    p_in = pltpu.make_async_copy(pt_ref, praw, in_sem.at[1])
    q_in.start()
    p_in.start()
    barrier = pltpu.get_barrier_semaphore()

    def greet_col(i, carry):
        pl.semaphore_signal(barrier, inc=1, device_id={"col": lax.rem(c + i, C)}, device_id_type=MESH)
        return carry

    def greet_row(i, carry):
        pl.semaphore_signal(barrier, inc=1, device_id={"row": lax.rem(r + i, R)}, device_id_type=MESH)
        return carry

    lax.fori_loop(1, C, greet_col, 0)
    lax.fori_loop(1, R, greet_row, 0)

    rows_p = lax.broadcasted_iota(jnp.int32, (PB, 128), 0)
    lane = lax.broadcasted_iota(jnp.int32, (1, 128), 1)
    lane_group = lax.div(lane, QB)

    def eye(n):
        a = lax.broadcasted_iota(jnp.int32, (n, n), 0)
        b = lax.broadcasted_iota(jnp.int32, (n, n), 1)
        return a, b

    a24, b24 = eye(24)
    sq_t = nt((a24 == b24).astype(BF), jnp.concatenate([sq_ref[...]] * GROUPS, axis=0))
    packed = jnp.zeros((8, 128), F32)
    for g in range(3):
        packed = jnp.where(lane_group == g, sq_t[8 * g : 8 * g + 8], packed)
    sqx[c] = packed
    aD, bD = eye(DR)
    source = lax.rem(lax.div(aD, 8), PR) * 24 + lax.div(aD, 8 * PR) * 8 + lax.rem(aD, 8)
    sp32 = sp_ref[...].astype(F32)
    sp_perm = jnp.concatenate(
        [sp32[8 * (2 * zz + kk) : 8 * (2 * zz + kk) + 8] for kk in range(2) for zz in range(Z)], axis=0
    ).astype(BF)
    spt[k, z] = nt((source == bD).astype(BF), sp_perm).astype(BF)

    q_in.wait()
    slot = lax.broadcasted_iota(jnp.int32, (L, 128), 0)
    q32 = jnp.stack(
        [jnp.where(slot < qlen_ref[i], qraw[i].astype(F32), 0.0) for i in range(QB)], axis=0
    )
    qbuf[r] = jnp.swapaxes(q32, 0, 1).reshape(N, 128).astype(BF)

    pl.semaphore_wait(barrier, C - 1 + R - 1)

    mine = pl.ds(pl.multiple_of(color * SL, SL), SL)
    mine_a = pl.ds(pl.multiple_of(color * SL, HALF), HALF)
    mine_b = pl.ds(pl.multiple_of(color * SL + HALF, HALF), HALF)

    def z_step(s):
        up = row_of(z - (s - 1), k)
        down = row_of(z + (s - 1), k)
        last = s == Z // 2
        a, b = (mine_a, mine_b) if last else (mine, mine)
        send(qbuf.at[up, a], qbuf.at[up, a], z_send.at[0, s - 1], z_recv.at[0, s - 1], row=row_of(z + 1, k))
        send(qbuf.at[down, b], qbuf.at[down, b], z_send.at[1, s - 1], z_recv.at[1, s - 1], row=row_of(z - 1, k))

    def z_got(s):
        last = s == Z // 2
        a, b = (mine_a, mine_b) if last else (mine, mine)
        got(qbuf.at[row_of(z - s, k), a], z_recv.at[0, s - 1])
        got(qbuf.at[row_of(z + s, k), b], z_recv.at[1, s - 1])

    offsets = []
    for s in range(1, Z // 2):
        offsets += [s, -s]
    offsets.append(Z // 2)

    def xy_regions():
        one = lax.rem(color + 3, 4) * SL
        two = lax.rem(color + 1, 4) * SL
        far = lax.rem(color + 2, 4) * SL
        return (
            pl.ds(pl.multiple_of(one, SL), SL),
            pl.ds(pl.multiple_of(two, SL), SL),
            pl.ds(pl.multiple_of(far, HALF), HALF),
            pl.ds(pl.multiple_of(far + HALF, HALF), HALF),
        )

    def xy_step(j):
        b = row_of(z + offsets[j], k)
        to = (col_of(x + 1, y), col_of(x - 1, y), col_of(x, y + 1), col_of(x, y - 1))
        for n, (part, peer) in enumerate(zip((mine, mine, mine_a, mine_b), to)):
            send(qbuf.at[b, part], qbuf.at[b, part], xy_send.at[n, j], xy_recv.at[n, j], col=peer)

    def xy_got(j):
        b = row_of(z + offsets[j], k)
        for n, part in enumerate(xy_regions()):
            got(qbuf.at[b, part], xy_recv.at[n, j])

    def sib_step(j):
        b = r if j == 0 else row_of(z + offsets[j - 1], k)
        send(qbuf.at[b], qbuf.at[b], sib_send.at[j], sib_recv.at[j], row=row_of(z, 1 - k))

    def sib_got(j):
        b = row_of(z, 1 - k) if j == 0 else row_of(z + offsets[j - 1], 1 - k)
        got(qbuf.at[b], sib_recv.at[j])
        return b

    def to_col(src_of, dst, n):
        def body(i, carry):
            peer = lax.rem(c + i, C)
            send(src_of(peer), dst, many_send.at[n], many_recv.at[n], col=peer)
            return carry

        lax.fori_loop(1, C, body, 0)

    def to_row(src_of, dst, n):
        def body(i, carry):
            peer = lax.rem(r + i, R)
            send(src_of(peer), dst, many_send.at[n], many_recv.at[n], row=peer)
            return carry

        lax.fori_loop(1, R, body, 0)

    def to_z(buf, n):
        def body(i, carry):
            send(buf.at[k, z], buf.at[k, z], many_send.at[n], many_recv.at[n], row=row_of(z + i, k))
            return carry

        lax.fori_loop(1, Z, body, 0)

    def z_to_sib(buf, n):
        got(buf.at[0, pl.ds(0, Z - 1)], many_recv.at[n])
        send(buf.at[k], buf.at[k], many_send.at[n + 1], many_recv.at[n + 1], row=row_of(z, 1 - k))

    z_step(1)
    sib_step(0)
    to_col(lambda peer: sqx.at[c], sqx.at[c], 0)
    to_z(spt, 1)

    p_in.wait()
    pslot = lax.broadcasted_iota(jnp.int32, (LP, 128), 0)
    p32 = []
    for i in range(8):
        rows = praw[i].astype(F32)
        p32.append(jnp.where(pslot < plen_ref[i], rows, rows[0:1]))
    xbuf[...] = jnp.swapaxes(jnp.stack(p32, axis=0), 0, 1).reshape(LP * 8, 128).astype(BF)

    def maxsim(b):
        s = nt(xbuf[...], qbuf[b])
        m = jnp.max(s.reshape(LP, 8, N), axis=0)
        acc = m[:, 0:128]
        for t in range(1, N // 128):
            acc = acc + m[:, 128 * t : 128 * t + 128]
        return spread(acc)

    def teach(blocks):
        found = [maxsim(b) for b in blocks]
        for b, v in zip(blocks, found):
            tblk[b] = v
            if b is r:
                town[k, z] = v
        for b in blocks:
            if b is not r:
                send(tblk.at[b], town.at[k, z], many_send.at[12], many_recv.at[12], row=b)

    def student_logits():
        got(sqx.at[pl.ds(0, C - 1)], many_recv.at[0])
        got(spt.at[1 - k], many_recv.at[2])
        part = jnp.zeros((PB, 128), F32)
        order = [PR * (2 * zz + kk) + u for kk in range(2) for zz in range(Z) for u in range(PR)]
        rhs = jnp.concatenate([sqx[i] for i in order], axis=0).astype(BF)
        aP, bP = eye(PB)
        unit = (aP == bP).astype(BF)
        for g in range(3):
            wide = spt[:, :, 8 * PR * g : 8 * PR * (g + 1), :].reshape(2 * Z * 8 * PR, PB)
            back = nt(unit, wide).astype(BF)
            part = jnp.where(lane_group == g, nn(back, rhs), part)
        sbuf[...] = SCALE * spread(part)

    rank = lax.div(rows_p, 8)
    p_index = c * PB + (2 * lax.rem(rank, Z) + lax.div(rank, Z)) * 8 + lax.rem(rows_p, 8)

    def onehot():
        wanted = jnp.zeros((1, 128), jnp.int32)
        within = lax.rem(lane, QB)
        for i in range(QB):
            wanted = jnp.where(within == i, pos_ref[i], wanted)
        return p_index == wanted

    def student_stats():
        s = sbuf[...]
        top = jnp.max(s, axis=0, keepdims=True)
        mass = jnp.sum(jnp.exp(s - top), axis=0, keepdims=True)
        hit = jnp.sum(jnp.where(onehot(), s, 0.0), axis=0, keepdims=True)
        sst[c] = jnp.where(lane_group == 0, top, jnp.where(lane_group == 1, mass, hit))
        to_col(lambda peer: sst.at[c], sst.at[c], 3)
        to_row(lambda peer: sqx.at[pl.ds(PR * peer, PR)], sqr.at[r], 4)
        sqr[r] = sqx[pl.ds(PR * r, PR)]

    def only(v, g):
        return spread(jnp.where(lane_group == g, v, 0.0))

    def pack(dst, weights, stats):
        hi, lo = split2(weights)
        u = nn(spt[...].reshape(2 * Z * DR, PB), jnp.concatenate([hi, lo], axis=1))
        u = u[:, 0:128] + u[:, 128:256]
        for kk in range(2):
            for zz in range(Z):
                for uu in range(PR):
                    base = (kk * Z + zz) * DR + 8 * uu
                    piece = stats
                    for g in range(3):
                        at = base + 8 * PR * g
                        piece = jnp.where(lane_group == g, u[at : at + 8], piece)
                    dst[PR * (2 * zz + kk) + uu] = piece

    def student_slopes():
        got(sst.at[pl.ds(0, C - 1)], many_recv.at[3])
        rows = [sst[i] for i in range(C)]
        top = only(functools.reduce(jnp.maximum, rows), 0)
        mass = jnp.zeros((1, 128), F32)
        hit = jnp.zeros((1, 128), F32)
        for v in rows:
            mass = mass + jnp.where(lane_group == 0, jnp.exp(jnp.minimum(v - top, 0.0)) * pltpu.roll(v, 96, 1), 0.0)
            hit = hit + v
        mass = spread(mass)
        hit = only(hit, 2)
        zz_ = 2.0 * (jnp.exp(sbuf[...] - top) / mass) - jnp.where(onehot(), 1.0, 0.0)
        pack(upz, zz_, jnp.zeros((8, 128), F32))
        vbuf[c] = upz[c]
        to_col(lambda peer: upz.at[peer], vbuf.at[c], 5)
        quarter = PB // GROUPS
        small = jnp.zeros((quarter, 128), F32)
        for g in range(GROUPS):
            small = jnp.where(lane_group == g, zz_[quarter * g : quarter * (g + 1)], small)
        zag[k, z] = small
        to_z(zag, 6)
        return top + jnp.log(mass), hit

    def unpack_slopes():
        got(zag.at[1 - k], many_recv.at[7])
        quarter = PB // GROUPS
        for t in range(T):
            for g in range(GROUPS):
                tile = jnp.zeros((quarter, 128), F32)
                for b in range(GROUPS):
                    rr = GROUPS * t + b
                    v = zag[rr % 2, rr // 2]
                    if b != g:
                        v = pltpu.roll(v, ((b - g) % GROUPS) * QB, 1)
                    tile = jnp.where(lane_group == b, v, tile)
                zfull[t, quarter * g : quarter * (g + 1)] = tile

    def unpack_queries():
        got(sqr.at[pl.ds(0, R - 1)], many_recv.at[4])
        tiles = []
        for t in range(T):
            rows = []
            for u in range(PR):
                for g in range(3):
                    tile = jnp.zeros((8, 128), F32)
                    for b in range(GROUPS):
                        v = sqr[GROUPS * t + b, u]
                        if b != g:
                            v = pltpu.roll(v, ((b - g) % GROUPS) * QB, 1)
                        tile = jnp.where(lane_group == b, v, tile)
                    rows.append(tile)
            tiles.append(jnp.concatenate(rows, axis=0).astype(BF))
        return tiles

    other = sib_got(0)
    teach([r, other])
    z_got(1)
    if Z // 2 > 1:
        z_step(2)
    z_to_sib(spt, 1)
    first = [j for j in range(len(offsets)) if abs(offsets[j]) == 1]
    for j in first:
        xy_step(j)
    student_logits()
    student_stats()
    kept = None
    for s in range(1, Z // 2 + 1):
        js = [j for j in range(len(offsets)) if abs(offsets[j]) == s]
        for j in js:
            xy_got(j)
            sib_step(j + 1)
        if s < Z // 2:
            z_got(s + 1)
            if s + 1 < Z // 2:
                z_step(s + 2)
            for j in range(len(offsets)):
                if abs(offsets[j]) == s + 1:
                    xy_step(j)
        if s < Z // 2:
            teach([row_of(z + offsets[j], k) for j in js])
            if s == 1:
                kept = student_slopes()
            if s == 2:
                z_to_sib(zag, 6)
            teach([sib_got(j + 1) for j in js])
        else:
            if kept is None:
                kept = student_slopes()
            if s <= 2:
                z_to_sib(zag, 6)
            unpack_slopes()
            teach([row_of(z + offsets[js[0]], k), sib_got(js[0] + 1)])
    student_lse, hit = kept

    for t in range(T):
        tile = tblk[GROUPS * t]
        for b in range(1, GROUPS):
            tile = jnp.where(lane_group == b, tblk[GROUPS * t + b], tile)
        tag[k, z, t] = tile
    to_z(tag, 8)
    got(tblk.at[pl.ds(0, R - 1)], many_recv.at[12])
    t_own = town[...].reshape(PB, 128)
    top = jnp.max(t_own, axis=0, keepdims=True)
    e = jnp.exp(t_own - top)
    mass = jnp.sum(e, axis=0, keepdims=True)
    cross = jnp.sum(e * (t_own - sbuf[...]), axis=0, keepdims=True)
    row8 = lax.broadcasted_iota(jnp.int32, (8, 128), 0)
    pack(upt, e, jnp.where(row8 == 0, top, jnp.where(row8 == 1, mass, cross)))
    ubuf[c] = upt[c]
    to_col(lambda peer: upt.at[peer], ubuf.at[c], 10)
    z_to_sib(tag, 8)
    sq_tiles = unpack_queries()
    got(vbuf.at[pl.ds(0, C - 1)], many_recv.at[5])
    v_sum = functools.reduce(jnp.add, [vbuf[i] for i in range(C)])

    got(ubuf.at[pl.ds(0, C - 1)], many_recv.at[10])
    highest = functools.reduce(jnp.maximum, [ubuf[i] for i in range(C)])
    top = only(highest, 3)[0:1]
    acc = jnp.zeros((8, 128), F32)
    for i in range(C):
        v = ubuf[i]
        w = only(jnp.exp(jnp.minimum(v[0:1] - top, 0.0)), 3)
        acc = acc + w * v
    whole = only(acc, 3)
    mass, cross = whole[1:2], whole[2:3]
    inverse = 1.0 / mass
    qg_ref[...] = (SCALE / total) * (v_sum - acc * inverse)
    per_query = cross * inverse - (top + jnp.log(mass)) + 2.0 * student_lse - hit
    fin[r] = jnp.where(lane_group == 0, top, jnp.where(lane_group == 1, inverse, per_query))
    to_row(lambda peer: fin.at[r], fin.at[r], 11)
    got(tag.at[1 - k], many_recv.at[9])

    got(fin.at[pl.ds(0, R - 1)], many_recv.at[11])
    grads = jnp.zeros((PB, DR), F32)
    per_query = jnp.zeros((1, 128), F32)
    for t in range(T):
        tops = jnp.zeros((1, 128), F32)
        inverses = jnp.zeros((1, 128), F32)
        for b in range(GROUPS):
            v = fin[GROUPS * t + b]
            per_query = per_query + jnp.where(lane_group == 2, v, 0.0)
            tops = jnp.where(lane_group == b, pltpu.roll(v, b * QB, 1) if b else v, tops)
            inverses = jnp.where(lane_group == b, pltpu.roll(v, ((b - 1) % GROUPS) * QB, 1) if b != 1 else v, inverses)
        probs = jnp.exp(tag[:, :, t].reshape(PB, 128) - tops) * inverses
        hi, lo = split2(zfull[t] - probs)
        grads = grads + nt(hi, sq_tiles[t]) + nt(lo, sq_tiles[t])
    grads = grads * (SCALE / total)
    for kk in range(2):
        for zz in range(Z):
            pg_ref[8 * (2 * zz + kk) : 8 * (2 * zz + kk) + 8, :] = grads[8 * (kk * Z + zz) : 8 * (kk * Z + zz) + 8]
    loss_ref[...] = jnp.zeros((1, 128), F32) + jnp.sum(per_query) / total

    for s in range(1, Z // 2 + 1):
        last = s == Z // 2
        a, b = (mine_a, mine_b) if last else (mine, mine)
        left(qbuf.at[row_of(z - (s - 1), k), a], z_send.at[0, s - 1])
        left(qbuf.at[row_of(z + (s - 1), k), b], z_send.at[1, s - 1])
    for j in range(len(offsets)):
        b = row_of(z + offsets[j], k)
        for n, part in enumerate((mine, mine, mine_a, mine_b)):
            left(qbuf.at[b, part], xy_send.at[n, j])
    for j in range(len(offsets) + 1):
        left(qbuf.at[r], sib_send.at[j])
    for n, buf, count in ((0, sqx, C), (3, sst, C), (5, upz, C), (10, upt, C), (4, sqr, R), (11, fin, R), (12, tblk, R)):
        left(buf.at[pl.ds(0, count - 1)], many_send.at[n])
    for n, buf in ((1, spt), (6, zag), (8, tag)):
        left(buf.at[0, pl.ds(0, Z - 1)], many_send.at[n])
        left(buf.at[0], many_send.at[n + 1])


def shards(query_tokens, query_lengths, passage_tokens, passage_lengths, student_queries, student_passages, positives):
    R = lax.axis_size("row")
    C = lax.axis_size("col")
    Z = R // 2
    L = query_tokens.shape[1]
    LP = passage_tokens.shape[1]
    PB = 8 * R
    PR = C // R
    DR = student_passages.shape[1]
    T = R // GROUPS
    hops = Z - 1
    dma = pltpu.SemaphoreType.DMA
    vmem = pl.BlockSpec(memory_space=pltpu.VMEM)
    smem = pl.BlockSpec(memory_space=pltpu.SMEM)
    anywhere = pl.BlockSpec(memory_space=pl.ANY)
    pg, qg, loss = pl.pallas_call(
        functools.partial(kernel, R, C),
        out_shape=(
            jax.ShapeDtypeStruct((PB, DR), F32),
            jax.ShapeDtypeStruct((8, 128), F32),
            jax.ShapeDtypeStruct((1, 128), F32),
        ),
        in_specs=[anywhere, smem, anywhere, smem, vmem, vmem, smem],
        out_specs=(vmem, vmem, vmem),
        scratch_shapes=[
            pltpu.VMEM((QB, L, 128), BF),
            pltpu.VMEM((8, LP, 128), BF),
            pltpu.VMEM((R, QB * L, 128), BF),
            pltpu.VMEM((LP * 8, 128), BF),
            pltpu.VMEM((C, 8, 128), F32),
            pltpu.VMEM((2, Z, DR, PB), BF),
            pltpu.VMEM((C, 1, 128), F32),
            pltpu.VMEM((PB, 128), F32),
            pltpu.VMEM((C, 8, 128), F32),
            pltpu.VMEM((C, 8, 128), F32),
            pltpu.VMEM((2, Z, PB // GROUPS, 128), F32),
            pltpu.VMEM((T, PB, 128), F32),
            pltpu.VMEM((R, PR, 8, 128), F32),
            pltpu.VMEM((R, 8, 128), F32),
            pltpu.VMEM((2, Z, 8, 128), F32),
            pltpu.VMEM((2, Z, T, 8, 128), F32),
            pltpu.VMEM((C, 8, 128), F32),
            pltpu.VMEM((C, 8, 128), F32),
            pltpu.VMEM((R, 1, 128), F32),
            dma((2,)),
            dma((2, Z // 2)),
            dma((2, Z // 2)),
            dma((4, hops)),
            dma((4, hops)),
            dma((hops + 1,)),
            dma((hops + 1,)),
            dma((13,)),
            dma((13,)),
        ],
        compiler_params=pltpu.CompilerParams(
            collective_id=0, has_side_effects=True, vmem_limit_bytes=48 * 1024 * 1024
        ),
        name="distill",
    )(query_tokens, query_lengths, passage_tokens, passage_lengths, student_queries, student_passages, positives)
    qg = qg.reshape(8, GROUPS, QB)[:, :3].transpose(2, 1, 0).reshape(QB, 24)
    return qg, pg, loss[0, 0]


def solution(mesh):
    return jax.shard_map(
        shards,
        mesh=mesh,
        in_specs=(
            P("row", None, None),
            P("row"),
            P(("col", "row"), None, None),
            P(("col", "row")),
            P("row", "col"),
            P("col", "row"),
            P("row"),
        ),
        out_specs=(P("row", "col"), P("col", "row"), P()),
        check_vma=False,
    )
```

```python
import functools

import jax
import jax.numpy as jnp
from jax import lax
from jax.experimental import pallas as pl
from jax.experimental.pallas import tpu as pltpu
from jax.sharding import PartitionSpec as P

MESH = pl.DeviceIdType.MESH
SCALE = 4.0
X_CHIPS = 4
QB = 32
GROUPS = 128 // QB
BF = jnp.bfloat16
F32 = jnp.float32


def nt(a, b):
    return lax.dot_general(a, b, (((1,), (1,)), ((), ())), preferred_element_type=F32)


def nn(a, b):
    return lax.dot_general(a, b, (((1,), (0,)), ((), ())), preferred_element_type=F32)


def split2(v):
    hi = v.astype(BF)
    return hi, (v - hi.astype(F32)).astype(BF)


def spread(v):
    v = v + pltpu.roll(v, 64, 1)
    return v + pltpu.roll(v, 32, 1)


def kernel(
    R,
    C,
    qt_hbm,
    qlen_hbm,
    pt_hbm,
    plen_hbm,
    sq_hbm,
    sp_hbm,
    pos_hbm,
    pg_ref,
    qg_ref,
    loss_ref,
    qlen_ref,
    plen_ref,
    pos_ref,
    sq_ref,
    sp_ref,
    qraw,
    praw,
    qbuf,
    xbuf,
    sqx,
    spt,
    sst,
    sbuf,
    upz,
    vbuf,
    zag,
    zfull,
    sqr,
    tblk,
    town,
    tag,
    upt,
    ubuf,
    fin,
    in_sem,
    z_send,
    z_recv,
    xy_send,
    xy_recv,
    sib_send,
    sib_recv,
    many_send,
    many_recv,
):
    Z = R // 2
    XC = min(X_CHIPS, C)
    YC = C // XC
    L = qt_hbm.shape[1]
    LP = pt_hbm.shape[1]
    N = QB * L
    SL = N // 4
    HALF = SL // 2
    PB = 8 * R
    PR = C // R
    DR = 24 * PR
    T = R // GROUPS
    total = QB * R

    r = lax.axis_index("row")
    c = lax.axis_index("col")
    z = lax.div(r, 2)
    k = lax.rem(r, 2)
    x = lax.rem(c, XC)
    y = lax.div(c, XC)
    color = lax.rem(x + 2 * y, 4)

    def row_of(zz, kk):
        return lax.rem(zz + 2 * Z, Z) * 2 + kk

    def col_of(xx, yy):
        return lax.rem(yy + YC, YC) * XC + lax.rem(xx + XC, XC)

    def send(src, dst, s_sem, r_sem, **where):
        pltpu.make_async_remote_copy(
            src_ref=src, dst_ref=dst, send_sem=s_sem, recv_sem=r_sem, device_id=where, device_id_type=MESH
        ).start()

    def got(dst, r_sem):
        pltpu.make_async_remote_copy(
            src_ref=dst, dst_ref=dst, send_sem=r_sem, recv_sem=r_sem, device_id={"row": r}, device_id_type=MESH
        ).wait_recv()

    def left(src, s_sem):
        pltpu.make_async_remote_copy(
            src_ref=src, dst_ref=src, send_sem=s_sem, recv_sem=s_sem, device_id={"row": r}, device_id_type=MESH
        ).wait_send()

    barrier = pltpu.get_barrier_semaphore()

    def greet_col(i, carry):
        pl.semaphore_signal(barrier, inc=1, device_id={"col": lax.rem(c + i, C)}, device_id_type=MESH)
        return carry

    def greet_row(i, carry):
        pl.semaphore_signal(barrier, inc=1, device_id={"row": lax.rem(r + i, R)}, device_id_type=MESH)
        return carry

    inputs = [
        pltpu.make_async_copy(src, dst, in_sem.at[n])
        for n, (src, dst) in enumerate(
            (
                (qt_hbm, qraw),
                (qlen_hbm, qlen_ref),
                (pt_hbm, praw),
                (plen_hbm, plen_ref),
                (sq_hbm, sq_ref),
                (sp_hbm, sp_ref),
                (pos_hbm, pos_ref),
            )
        )
    ]
    for copy in inputs:
        copy.start()
    lax.fori_loop(1, R, greet_row, 0)
    lax.fori_loop(1, C, greet_col, 0)

    rows_p = lax.broadcasted_iota(jnp.int32, (PB, 128), 0)
    lane = lax.broadcasted_iota(jnp.int32, (1, 128), 1)
    lane_group = lax.div(lane, QB)

    def natural(i):
        rank = lax.div(i, 8)
        return (2 * lax.rem(rank, Z) + lax.div(rank, Z)) * 8 + lax.rem(i, 8)

    inputs[0].wait()
    inputs[1].wait()
    slot = lax.broadcasted_iota(jnp.int32, (L, 128), 0)
    q32 = jnp.stack(
        [jnp.where(slot < qlen_ref[i], qraw[i].astype(F32), 0.0) for i in range(QB)], axis=0
    )
    qbuf[r] = jnp.swapaxes(q32, 0, 1).reshape(N, 128).astype(BF)

    inputs[4].wait()
    inputs[5].wait()
    qa = lax.broadcasted_iota(jnp.int32, (QB, 128), 0)
    qb = lax.broadcasted_iota(jnp.int32, (QB, 128), 1)
    sq_wide = nn(sq_ref[...], (qa == lax.rem(qb, QB)).astype(BF))
    packed = jnp.zeros((8, 128), F32)
    for g in range(3):
        packed = jnp.where(lane_group == g, sq_wide[8 * g : 8 * g + 8], packed)
    sqx[c] = packed
    pa = lax.broadcasted_iota(jnp.int32, (PB, PB), 0)
    pb = lax.broadcasted_iota(jnp.int32, (PB, PB), 1)
    sp_wide = nn(sp_ref[...], (pa == natural(pb)).astype(BF))
    spt[k, z] = jnp.concatenate(
        [sp_wide[24 * u + 8 * g : 24 * u + 8 * g + 8] for g in range(3) for u in range(PR)], axis=0
    ).astype(BF)

    inputs[2].wait()
    inputs[3].wait()
    inputs[6].wait()
    pslot = lax.broadcasted_iota(jnp.int32, (LP, 128), 0)
    p32 = []
    for i in range(8):
        rows = praw[i].astype(F32)
        p32.append(jnp.where(pslot < plen_ref[i], rows, rows[0:1]))
    xbuf[...] = jnp.swapaxes(jnp.stack(p32, axis=0), 0, 1).reshape(LP * 8, 128).astype(BF)

    def maxsim(b):
        s = nt(xbuf[...], qbuf[b])
        m = jnp.max(s.reshape(LP, 8, N), axis=0)
        acc = m[:, 0:128]
        for t in range(1, N // 128):
            acc = acc + m[:, 128 * t : 128 * t + 128]
        return spread(acc)

    def teach(blocks):
        found = [maxsim(b) for b in blocks]
        for b, v in zip(blocks, found):
            tblk[b] = v
        for b in blocks:
            send(tblk.at[b], town.at[k, z], many_send.at[12], many_recv.at[12], row=b)

    own = maxsim(r)
    tblk[r] = own
    town[k, z] = own

    pl.semaphore_wait(barrier, C - 1 + R - 1)

    mine = pl.ds(pl.multiple_of(color * SL, SL), SL)
    mine_a = pl.ds(pl.multiple_of(color * SL, HALF), HALF)
    mine_b = pl.ds(pl.multiple_of(color * SL + HALF, HALF), HALF)

    def z_step(s):
        up = row_of(z - (s - 1), k)
        down = row_of(z + (s - 1), k)
        last = s == Z // 2
        a, b = (mine_a, mine_b) if last else (mine, mine)
        send(qbuf.at[up, a], qbuf.at[up, a], z_send.at[0, s - 1], z_recv.at[0, s - 1], row=row_of(z + 1, k))
        send(qbuf.at[down, b], qbuf.at[down, b], z_send.at[1, s - 1], z_recv.at[1, s - 1], row=row_of(z - 1, k))

    def z_got(s):
        last = s == Z // 2
        a, b = (mine_a, mine_b) if last else (mine, mine)
        got(qbuf.at[row_of(z - s, k), a], z_recv.at[0, s - 1])
        got(qbuf.at[row_of(z + s, k), b], z_recv.at[1, s - 1])

    offsets = []
    for s in range(1, Z // 2):
        offsets += [s, -s]
    offsets.append(Z // 2)

    def xy_regions():
        one = lax.rem(color + 3, 4) * SL
        two = lax.rem(color + 1, 4) * SL
        far = lax.rem(color + 2, 4) * SL
        return (
            pl.ds(pl.multiple_of(one, SL), SL),
            pl.ds(pl.multiple_of(two, SL), SL),
            pl.ds(pl.multiple_of(far, HALF), HALF),
            pl.ds(pl.multiple_of(far + HALF, HALF), HALF),
        )

    def xy_step(j):
        b = row_of(z + offsets[j], k)
        to = (col_of(x + 1, y), col_of(x - 1, y), col_of(x, y + 1), col_of(x, y - 1))
        for n, (part, peer) in enumerate(zip((mine, mine, mine_a, mine_b), to)):
            send(qbuf.at[b, part], qbuf.at[b, part], xy_send.at[n, j], xy_recv.at[n, j], col=peer)

    def xy_got(j):
        b = row_of(z + offsets[j], k)
        for n, part in enumerate(xy_regions()):
            got(qbuf.at[b, part], xy_recv.at[n, j])

    def sib_step(j):
        b = r if j == 0 else row_of(z + offsets[j - 1], k)
        send(qbuf.at[b], qbuf.at[b], sib_send.at[j], sib_recv.at[j], row=row_of(z, 1 - k))

    def sib_got(j):
        b = row_of(z, 1 - k) if j == 0 else row_of(z + offsets[j - 1], 1 - k)
        got(qbuf.at[b], sib_recv.at[j])
        return b

    def to_col(src_of, dst, n):
        def body(i, carry):
            peer = lax.rem(c + i, C)
            send(src_of(peer), dst, many_send.at[n], many_recv.at[n], col=peer)
            return carry

        lax.fori_loop(1, C, body, 0)

    def to_row(src_of, dst, n):
        def body(i, carry):
            peer = lax.rem(r + i, R)
            send(src_of(peer), dst, many_send.at[n], many_recv.at[n], row=peer)
            return carry

        lax.fori_loop(1, R, body, 0)

    def to_z(buf, n):
        def body(i, carry):
            send(buf.at[k, z], buf.at[k, z], many_send.at[n], many_recv.at[n], row=row_of(z + i, k))
            return carry

        lax.fori_loop(1, Z, body, 0)

    def z_to_sib(buf, n):
        got(buf.at[0, pl.ds(0, Z - 1)], many_recv.at[n])
        send(buf.at[k], buf.at[k], many_send.at[n + 1], many_recv.at[n + 1], row=row_of(z, 1 - k))

    z_step(1)
    sib_step(0)
    to_col(lambda peer: sqx.at[c], sqx.at[c], 0)
    to_z(spt, 1)

    def student_logits():
        got(sqx.at[pl.ds(0, C - 1)], many_recv.at[0])
        got(spt.at[1 - k], many_recv.at[2])
        part = jnp.zeros((PB, 128), F32)
        order = [PR * (2 * zz + kk) + u for kk in range(2) for zz in range(Z) for u in range(PR)]
        rhs = jnp.concatenate([sqx[i] for i in order], axis=0).astype(BF)
        unit = (pa == pb).astype(BF)
        for g in range(3):
            wide = spt[:, :, 8 * PR * g : 8 * PR * (g + 1), :].reshape(2 * Z * 8 * PR, PB)
            back = nt(unit, wide).astype(BF)
            part = jnp.where(lane_group == g, nn(back, rhs), part)
        sbuf[...] = SCALE * spread(part)

    p_index = c * PB + natural(rows_p)

    def onehot():
        wanted = jnp.zeros((1, 128), jnp.int32)
        within = lax.rem(lane, QB)
        for i in range(QB):
            wanted = jnp.where(within == i, pos_ref[i], wanted)
        return p_index == wanted

    def student_stats():
        s = sbuf[...]
        top = jnp.max(s, axis=0, keepdims=True)
        mass = jnp.sum(jnp.exp(s - top), axis=0, keepdims=True)
        hit = jnp.sum(jnp.where(onehot(), s, 0.0), axis=0, keepdims=True)
        sst[c] = jnp.where(lane_group == 0, top, jnp.where(lane_group == 1, mass, hit))
        to_col(lambda peer: sst.at[c], sst.at[c], 3)
        to_row(lambda peer: sqx.at[pl.ds(PR * peer, PR)], sqr.at[r], 4)
        sqr[r] = sqx[pl.ds(PR * r, PR)]

    def only(v, g):
        return spread(jnp.where(lane_group == g, v, 0.0))

    def pack(dst, weights, stats):
        hi, lo = split2(weights)
        table = spt[...].reshape(2 * Z * DR, PB)
        u = nn(jnp.concatenate([table, table], axis=1), jnp.concatenate([hi, lo], axis=0))
        for kk in range(2):
            for zz in range(Z):
                for uu in range(PR):
                    base = (kk * Z + zz) * DR + 8 * uu
                    piece = stats
                    for g in range(3):
                        at = base + 8 * PR * g
                        piece = jnp.where(lane_group == g, u[at : at + 8], piece)
                    dst[PR * (2 * zz + kk) + uu] = piece

    def student_slopes():
        got(sst.at[pl.ds(0, C - 1)], many_recv.at[3])
        rows = [sst[i] for i in range(C)]
        top = only(functools.reduce(jnp.maximum, rows), 0)
        mass = jnp.zeros((1, 128), F32)
        hit = jnp.zeros((1, 128), F32)
        for v in rows:
            mass = mass + jnp.where(lane_group == 0, jnp.exp(jnp.minimum(v - top, 0.0)) * pltpu.roll(v, 96, 1), 0.0)
            hit = hit + v
        mass = spread(mass)
        hit = only(hit, 2)
        zz_ = 2.0 * (jnp.exp(sbuf[...] - top) / mass) - jnp.where(onehot(), 1.0, 0.0)
        pack(upz, zz_, jnp.zeros((8, 128), F32))
        vbuf[c] = upz[c]
        to_col(lambda peer: upz.at[peer], vbuf.at[c], 5)
        quarter = PB // GROUPS
        small = jnp.zeros((quarter, 128), F32)
        for g in range(GROUPS):
            small = jnp.where(lane_group == g, zz_[quarter * g : quarter * (g + 1)], small)
        zag[k, z] = small
        to_z(zag, 6)
        return top + jnp.log(mass), hit

    def unpack_slopes():
        got(zag.at[1 - k], many_recv.at[7])
        quarter = PB // GROUPS
        for t in range(T):
            for g in range(GROUPS):
                tile = jnp.zeros((quarter, 128), F32)
                for b in range(GROUPS):
                    rr = GROUPS * t + b
                    v = zag[rr % 2, rr // 2]
                    if b != g:
                        v = pltpu.roll(v, ((b - g) % GROUPS) * QB, 1)
                    tile = jnp.where(lane_group == b, v, tile)
                zfull[t, quarter * g : quarter * (g + 1)] = tile

    def unpack_queries():
        got(sqr.at[pl.ds(0, R - 1)], many_recv.at[4])
        tiles = []
        for t in range(T):
            rows = []
            for u in range(PR):
                for g in range(3):
                    tile = jnp.zeros((8, 128), F32)
                    for b in range(GROUPS):
                        v = sqr[GROUPS * t + b, u]
                        if b != g:
                            v = pltpu.roll(v, ((b - g) % GROUPS) * QB, 1)
                        tile = jnp.where(lane_group == b, v, tile)
                    rows.append(tile)
            tiles.append(jnp.concatenate(rows, axis=0).astype(BF))
        return tiles

    half = Z // 2

    def at(s, kk):
        return [row_of(z + o, kk) for o in offsets if abs(o) == s]

    def numbers(s):
        return [j for j, o in enumerate(offsets) if abs(o) == s]

    def z_turn(s):
        z_got(s)
        if s < half:
            z_step(s + 1)
        for j in numbers(s):
            xy_step(j)

    def whole(s):
        for j in numbers(s):
            xy_got(j)
            sib_step(j + 1)

    def handed(s):
        for j in numbers(s):
            sib_got(j + 1)

    teach([sib_got(0)])
    z_turn(1)
    z_to_sib(spt, 1)
    if half >= 2:
        z_turn(2)
    whole(1)
    if half >= 2:
        teach(at(1, k))
        if half >= 3:
            z_turn(3)
        student_logits()
        student_stats()
        for s in range(2, half + 1):
            whole(s)
            if s + 2 <= half:
                z_turn(s + 2)
            if s < half:
                teach(at(s, k))
                handed(s)
                teach(at(s, 1 - k))
            else:
                handed(s)
                teach(at(s, k) + at(s, 1 - k))
        handed(1)
        teach(at(1, 1 - k))
    else:
        student_logits()
        student_stats()
        handed(1)
        teach(at(1, k) + at(1, 1 - k))

    for t in range(T):
        tile = tblk[GROUPS * t]
        for b in range(1, GROUPS):
            tile = jnp.where(lane_group == b, tblk[GROUPS * t + b], tile)
        tag[k, z, t] = tile
    to_z(tag, 8)
    student_lse, hit = student_slopes()
    got(tblk.at[pl.ds(0, R - 1)], many_recv.at[12])
    t_own = town[...].reshape(PB, 128)
    top = jnp.max(t_own, axis=0, keepdims=True)
    e = jnp.exp(t_own - top)
    mass = jnp.sum(e, axis=0, keepdims=True)
    cross = jnp.sum(e * (t_own - sbuf[...]), axis=0, keepdims=True)
    row8 = lax.broadcasted_iota(jnp.int32, (8, 128), 0)
    pack(upt, e, jnp.where(row8 == 0, top, jnp.where(row8 == 1, mass, cross)))
    ubuf[c] = upt[c]
    to_col(lambda peer: upt.at[peer], ubuf.at[c], 10)
    z_to_sib(zag, 6)
    sq_tiles = unpack_queries()
    got(vbuf.at[pl.ds(0, C - 1)], many_recv.at[5])
    v_sum = functools.reduce(jnp.add, [vbuf[i] for i in range(C)])

    got(ubuf.at[pl.ds(0, C - 1)], many_recv.at[10])
    tops = only(jnp.concatenate([ubuf[i, 0:1] for i in range(C)], axis=0), 3)
    top = jnp.max(tops, axis=0, keepdims=True)
    weights = jnp.exp(tops - top)
    acc = jnp.zeros((8, 128), F32)
    for i in range(C):
        acc = acc + weights[i : i + 1] * ubuf[i]
    whole = only(acc, 3)
    mass, cross = whole[1:2], whole[2:3]
    inverse = 1.0 / mass
    grads = (SCALE / total) * (v_sum - acc * inverse)
    for g in range(3):
        qg_ref[8 * g : 8 * g + 8, :] = (pltpu.roll(grads, 128 - QB * g, 1) if g else grads)[:, 0:QB]
    per_query = cross * inverse - (top + jnp.log(mass)) + 2.0 * student_lse - hit
    fin[r] = jnp.where(lane_group == 0, top, jnp.where(lane_group == 1, inverse, per_query))
    to_row(lambda peer: fin.at[r], fin.at[r], 11)
    z_to_sib(tag, 8)
    unpack_slopes()
    got(tag.at[1 - k], many_recv.at[9])

    got(fin.at[pl.ds(0, R - 1)], many_recv.at[11])
    grads = jnp.zeros((DR, PB), F32)
    per_query = jnp.zeros((1, 128), F32)
    for t in range(T):
        tops = jnp.zeros((1, 128), F32)
        inverses = jnp.zeros((1, 128), F32)
        for b in range(GROUPS):
            v = fin[GROUPS * t + b]
            per_query = per_query + jnp.where(lane_group == 2, v, 0.0)
            tops = jnp.where(lane_group == b, pltpu.roll(v, b * QB, 1) if b else v, tops)
            inverses = jnp.where(lane_group == b, pltpu.roll(v, ((b - 1) % GROUPS) * QB, 1) if b != 1 else v, inverses)
        slopes = zfull[t] - jnp.exp(tag[:, :, t].reshape(PB, 128) - tops) * inverses
        slopes = jnp.concatenate(
            [slopes[8 * (kk * Z + zz) : 8 * (kk * Z + zz) + 8] for zz in range(Z) for kk in range(2)], axis=0
        )
        hi, lo = split2(slopes)
        grads = grads + nt(jnp.concatenate([sq_tiles[t]] * 2, axis=1), jnp.concatenate([hi, lo], axis=1))
    pg_ref[...] = grads * (SCALE / total)
    loss_ref[...] = jnp.zeros((1, 1), F32) + jnp.sum(per_query) / total

    for s in range(1, Z // 2 + 1):
        last = s == Z // 2
        a, b = (mine_a, mine_b) if last else (mine, mine)
        left(qbuf.at[row_of(z - (s - 1), k), a], z_send.at[0, s - 1])
        left(qbuf.at[row_of(z + (s - 1), k), b], z_send.at[1, s - 1])
    for j in range(len(offsets)):
        b = row_of(z + offsets[j], k)
        for n, part in enumerate((mine, mine, mine_a, mine_b)):
            left(qbuf.at[b, part], xy_send.at[n, j])
    for j in range(len(offsets) + 1):
        left(qbuf.at[r], sib_send.at[j])
    for n, buf, count in ((0, sqx, C), (3, sst, C), (5, upz, C), (10, upt, C), (4, sqr, R), (11, fin, R), (12, tblk, R)):
        left(buf.at[pl.ds(0, count - 1)], many_send.at[n])
    for n, buf in ((1, spt), (6, zag), (8, tag)):
        left(buf.at[0, pl.ds(0, Z - 1)], many_send.at[n])
        left(buf.at[0], many_send.at[n + 1])


def shards(query_tokens, query_lengths, passage_tokens, passage_lengths, student_queries, student_passages, positives):
    R = lax.axis_size("row")
    C = lax.axis_size("col")
    Z = R // 2
    L = query_tokens.shape[1]
    LP = passage_tokens.shape[1]
    PB = 8 * R
    PR = C // R
    DR = student_passages.shape[1]
    T = R // GROUPS
    hops = Z - 1
    dma = pltpu.SemaphoreType.DMA
    vmem = pl.BlockSpec(memory_space=pltpu.VMEM)
    hbm = pl.BlockSpec(memory_space=pltpu.HBM)
    pg, qg, loss = pl.pallas_call(
        functools.partial(kernel, R, C),
        out_shape=(
            jax.ShapeDtypeStruct((DR, PB), F32),
            jax.ShapeDtypeStruct((24, QB), F32),
            jax.ShapeDtypeStruct((1, 1), F32),
        ),
        in_specs=[hbm] * 7,
        out_specs=(vmem, vmem, vmem),
        scratch_shapes=[
            pltpu.SMEM((QB,), jnp.int32),
            pltpu.SMEM((8,), jnp.int32),
            pltpu.SMEM((QB,), jnp.int32),
            pltpu.VMEM((24, QB), BF),
            pltpu.VMEM((DR, PB), BF),
            pltpu.VMEM((QB, L, 128), BF),
            pltpu.VMEM((8, LP, 128), BF),
            pltpu.VMEM((R, QB * L, 128), BF),
            pltpu.VMEM((LP * 8, 128), BF),
            pltpu.VMEM((C, 8, 128), F32),
            pltpu.VMEM((2, Z, DR, PB), BF),
            pltpu.VMEM((C, 1, 128), F32),
            pltpu.VMEM((PB, 128), F32),
            pltpu.VMEM((C, 8, 128), F32),
            pltpu.VMEM((C, 8, 128), F32),
            pltpu.VMEM((2, Z, PB // GROUPS, 128), F32),
            pltpu.VMEM((T, PB, 128), F32),
            pltpu.VMEM((R, PR, 8, 128), F32),
            pltpu.VMEM((R, 8, 128), F32),
            pltpu.VMEM((2, Z, 8, 128), F32),
            pltpu.VMEM((2, Z, T, 8, 128), F32),
            pltpu.VMEM((C, 8, 128), F32),
            pltpu.VMEM((C, 8, 128), F32),
            pltpu.VMEM((R, 1, 128), F32),
            dma((7,)),
            dma((2, Z // 2)),
            dma((2, Z // 2)),
            dma((4, hops)),
            dma((4, hops)),
            dma((hops + 1,)),
            dma((hops + 1,)),
            dma((13,)),
            dma((13,)),
        ],
        compiler_params=pltpu.CompilerParams(
            collective_id=0, has_side_effects=True, vmem_limit_bytes=64 * 1024 * 1024
        ),
        name="distill",
    )(query_tokens, query_lengths, passage_tokens, passage_lengths, student_queries.T, student_passages.T, positives)
    return qg.T, pg.T, loss.reshape(())


def solution(mesh):
    return jax.shard_map(
        shards,
        mesh=mesh,
        in_specs=(
            P("row", None, None),
            P("row"),
            P(("col", "row"), None, None),
            P(("col", "row")),
            P("row", "col"),
            P("col", "row"),
            P("row"),
        ),
        out_specs=(P("row", "col"), P("col", "row"), P()),
        check_vma=False,
    )
```

```python
import functools

import jax
import jax.numpy as jnp
from jax import lax
from jax.experimental import pallas as pl
from jax.experimental.pallas import tpu as pltpu
from jax.sharding import PartitionSpec as P

MESH = pl.DeviceIdType.MESH
SCALE = 4.0
X_CHIPS = 4
QB = 32
GROUPS = 128 // QB
BF = jnp.bfloat16
F32 = jnp.float32


def nt(a, b):
    return lax.dot_general(a, b, (((1,), (1,)), ((), ())), preferred_element_type=F32)


def nn(a, b):
    return lax.dot_general(a, b, (((1,), (0,)), ((), ())), preferred_element_type=F32)


def split2(v):
    hi = v.astype(BF)
    return hi, (v - hi.astype(F32)).astype(BF)


def spread(v):
    v = v + pltpu.roll(v, 64, 1)
    return v + pltpu.roll(v, 32, 1)


def kernel(
    R,
    C,
    qt_hbm,
    qlen_hbm,
    pt_hbm,
    plen_hbm,
    sq_hbm,
    sp_hbm,
    pos_hbm,
    pg_ref,
    qg_ref,
    loss_ref,
    qlen_ref,
    plen_ref,
    pos_ref,
    sq_ref,
    sp_ref,
    qraw,
    praw,
    qbuf,
    xbuf,
    sqx,
    spt,
    sst,
    sbuf,
    upz,
    vbuf,
    zag,
    zfull,
    sqr,
    tblk,
    town,
    tag,
    upt,
    ubuf,
    fin,
    in_sem,
    z_send,
    z_recv,
    s_send,
    s_recv,
    x_send,
    x_recv,
    y_send,
    y_recv,
    xy_send,
    xy_recv,
    sib_send,
    sib_recv,
    many_send,
    many_recv,
):
    Z = R // 2
    XC = min(X_CHIPS, C)
    YC = C // XC
    L = qt_hbm.shape[1]
    LP = pt_hbm.shape[1]
    N = QB * L
    SL = N // 4
    HALF = SL // 2
    PB = 8 * R
    PR = C // R
    DR = 24 * PR
    T = R // GROUPS
    total = QB * R

    r = lax.axis_index("row")
    c = lax.axis_index("col")
    z = lax.div(r, 2)
    k = lax.rem(r, 2)
    x = lax.rem(c, XC)
    y = lax.div(c, XC)
    color = lax.rem(x + 2 * y, 4)

    def row_of(zz, kk):
        return lax.rem(zz + 2 * Z, Z) * 2 + kk

    def col_of(xx, yy):
        return lax.rem(yy + YC, YC) * XC + lax.rem(xx + XC, XC)

    def send(src, dst, s_sem, r_sem, **where):
        pltpu.make_async_remote_copy(
            src_ref=src, dst_ref=dst, send_sem=s_sem, recv_sem=r_sem, device_id=where, device_id_type=MESH
        ).start()

    def got(dst, r_sem):
        pltpu.make_async_remote_copy(
            src_ref=dst, dst_ref=dst, send_sem=r_sem, recv_sem=r_sem, device_id={"row": r}, device_id_type=MESH
        ).wait_recv()

    def left(src, s_sem):
        pltpu.make_async_remote_copy(
            src_ref=src, dst_ref=src, send_sem=s_sem, recv_sem=s_sem, device_id={"row": r}, device_id_type=MESH
        ).wait_send()

    barrier = pltpu.get_barrier_semaphore()

    neighbours = (
        {"row": row_of(z, 1 - k)},
        {"row": row_of(z + 1, k)},
        {"row": row_of(z - 1, k)},
        {"col": col_of(x + 1, y)},
        {"col": col_of(x - 1, y)},
        {"col": col_of(x, y + 1)},
        {"col": col_of(x, y - 1)},
    )
    for peer in neighbours:
        pl.semaphore_signal(barrier, inc=1, device_id=peer, device_id_type=MESH)

    inputs = [
        pltpu.make_async_copy(src, dst, in_sem.at[n])
        for n, (src, dst) in enumerate(
            (
                (qt_hbm, qraw),
                (qlen_hbm, qlen_ref),
                (pt_hbm, praw),
                (plen_hbm, plen_ref),
                (sq_hbm, sq_ref),
                (sp_hbm, sp_ref),
                (pos_hbm, pos_ref),
            )
        )
    ]
    for copy in inputs:
        copy.start()

    rows_p = lax.broadcasted_iota(jnp.int32, (PB, 128), 0)
    lane = lax.broadcasted_iota(jnp.int32, (1, 128), 1)
    lane_group = lax.div(lane, QB)

    def natural(i):
        rank = lax.div(i, 8)
        return (2 * lax.rem(rank, Z) + lax.div(rank, Z)) * 8 + lax.rem(i, 8)

    inputs[0].wait()
    inputs[1].wait()
    slot = lax.broadcasted_iota(jnp.int32, (L, 128), 0)
    q32 = jnp.stack(
        [jnp.where(slot < qlen_ref[i], qraw[i].astype(F32), 0.0) for i in range(QB)], axis=0
    )
    qbuf[r] = jnp.swapaxes(q32, 0, 1).reshape(N, 128).astype(BF)

    inputs[4].wait()
    inputs[5].wait()
    qa = lax.broadcasted_iota(jnp.int32, (QB, 128), 0)
    qb = lax.broadcasted_iota(jnp.int32, (QB, 128), 1)
    sq_wide = nn(sq_ref[...], (qa == lax.rem(qb, QB)).astype(BF))
    packed = jnp.zeros((8, 128), F32)
    for g in range(3):
        packed = jnp.where(lane_group == g, sq_wide[8 * g : 8 * g + 8], packed)
    sqx[c] = packed
    pa = lax.broadcasted_iota(jnp.int32, (PB, PB), 0)
    pb = lax.broadcasted_iota(jnp.int32, (PB, PB), 1)
    sp_wide = nn(sp_ref[...], (pa == natural(pb)).astype(BF))
    spt[k, z] = jnp.concatenate(
        [sp_wide[24 * u + 8 * g : 24 * u + 8 * g + 8] for g in range(3) for u in range(PR)], axis=0
    ).astype(BF)

    inputs[2].wait()
    inputs[3].wait()
    inputs[6].wait()
    pslot = lax.broadcasted_iota(jnp.int32, (LP, 128), 0)
    p32 = []
    for i in range(8):
        rows = praw[i].astype(F32)
        p32.append(jnp.where(pslot < plen_ref[i], rows, rows[0:1]))
    xbuf[...] = jnp.swapaxes(jnp.stack(p32, axis=0), 0, 1).reshape(LP * 8, 128).astype(BF)

    def maxsim(b):
        s = nt(xbuf[...], qbuf[b])
        m = jnp.max(s.reshape(LP, 8, N), axis=0)
        acc = m[:, 0:128]
        for t in range(1, N // 128):
            acc = acc + m[:, 128 * t : 128 * t + 128]
        return spread(acc)

    def teach(blocks):
        found = [maxsim(b) for b in blocks]
        for b, v in zip(blocks, found):
            tblk[b] = v
        for b in blocks:
            send(tblk.at[b], town.at[k, z], many_send.at[12], many_recv.at[12], row=b)

    own = maxsim(r)
    tblk[r] = own
    town[k, z] = own

    pl.semaphore_wait(barrier, len(neighbours))

    mine = pl.ds(pl.multiple_of(color * SL, SL), SL)
    mine_a = pl.ds(pl.multiple_of(color * SL, HALF), HALF)
    mine_b = pl.ds(pl.multiple_of(color * SL + HALF, HALF), HALF)

    def z_step(s):
        up = row_of(z - (s - 1), k)
        down = row_of(z + (s - 1), k)
        last = s == Z // 2
        a, b = (mine_a, mine_b) if last else (mine, mine)
        send(qbuf.at[up, a], qbuf.at[up, a], z_send.at[0, s - 1], z_recv.at[0, s - 1], row=row_of(z + 1, k))
        send(qbuf.at[down, b], qbuf.at[down, b], z_send.at[1, s - 1], z_recv.at[1, s - 1], row=row_of(z - 1, k))
        table = spt.at[k, lax.div(up, 2)]
        send(table, table, s_send.at[0, s - 1], s_recv.at[0, s - 1], row=row_of(z + 1, k))
        if not last:
            table = spt.at[k, lax.div(down, 2)]
            send(table, table, s_send.at[1, s - 1], s_recv.at[1, s - 1], row=row_of(z - 1, k))

    def z_got(s):
        last = s == Z // 2
        a, b = (mine_a, mine_b) if last else (mine, mine)
        got(qbuf.at[row_of(z - s, k), a], z_recv.at[0, s - 1])
        got(qbuf.at[row_of(z + s, k), b], z_recv.at[1, s - 1])
        got(spt.at[k, lax.div(row_of(z - s, k), 2)], s_recv.at[0, s - 1])
        if not last:
            got(spt.at[k, lax.div(row_of(z + s, k), 2)], s_recv.at[1, s - 1])

    offsets = []
    for s in range(1, Z // 2):
        offsets += [s, -s]
    offsets.append(Z // 2)

    def xy_regions():
        one = lax.rem(color + 3, 4) * SL
        two = lax.rem(color + 1, 4) * SL
        far = lax.rem(color + 2, 4) * SL
        return (
            pl.ds(pl.multiple_of(one, SL), SL),
            pl.ds(pl.multiple_of(two, SL), SL),
            pl.ds(pl.multiple_of(far, HALF), HALF),
            pl.ds(pl.multiple_of(far + HALF, HALF), HALF),
        )

    def xy_step(j):
        b = row_of(z + offsets[j], k)
        to = (col_of(x + 1, y), col_of(x - 1, y), col_of(x, y + 1), col_of(x, y - 1))
        for n, (part, peer) in enumerate(zip((mine, mine, mine_a, mine_b), to)):
            send(qbuf.at[b, part], qbuf.at[b, part], xy_send.at[n, j], xy_recv.at[n, j], col=peer)

    def xy_got(j):
        b = row_of(z + offsets[j], k)
        for n, part in enumerate(xy_regions()):
            got(qbuf.at[b, part], xy_recv.at[n, j])

    def sib_step(j):
        b = r if j == 0 else row_of(z + offsets[j - 1], k)
        send(qbuf.at[b], qbuf.at[b], sib_send.at[j], sib_recv.at[j], row=row_of(z, 1 - k))

    def sib_got(j):
        b = row_of(z, 1 - k) if j == 0 else row_of(z + offsets[j - 1], 1 - k)
        got(qbuf.at[b], sib_recv.at[j])
        return b

    def x_first():
        for n, peer in enumerate((col_of(x + 1, y), col_of(x - 1, y))):
            send(sqx.at[c], sqx.at[c], x_send.at[n], x_recv.at[n], col=peer)

    def x_second():
        back = col_of(x - 1, y)
        got(sqx.at[back], x_recv.at[0])
        send(sqx.at[back], sqx.at[back], x_send.at[2], x_recv.at[2], col=col_of(x + 1, y))

    def x_last():
        got(sqx.at[col_of(x + 1, y)], x_recv.at[1])
        got(sqx.at[col_of(x - 2, y)], x_recv.at[2])

    def chips(yy):
        return sqx.at[pl.ds(col_of(0, yy), XC)]

    def y_step(s):
        up, down = chips(y - (s - 1)), chips(y + (s - 1))
        send(up, up, y_send.at[0, s - 1], y_recv.at[0, s - 1], col=col_of(x, y + 1))
        if s < YC // 2:
            send(down, down, y_send.at[1, s - 1], y_recv.at[1, s - 1], col=col_of(x, y - 1))

    def y_turn(s):
        got(chips(y - s), y_recv.at[0, s - 1])
        if s < YC // 2:
            got(chips(y + s), y_recv.at[1, s - 1])
            y_step(s + 1)

    def x_last_and_y():
        x_last()
        y_step(1)

    def to_col(src_of, dst, n):
        def body(i, carry):
            peer = lax.rem(c + i, C)
            send(src_of(peer), dst, many_send.at[n], many_recv.at[n], col=peer)
            return carry

        lax.fori_loop(1, C, body, 0)

    def to_row(src_of, dst, n):
        def body(i, carry):
            peer = lax.rem(r + i, R)
            send(src_of(peer), dst, many_send.at[n], many_recv.at[n], row=peer)
            return carry

        lax.fori_loop(1, R, body, 0)

    def to_z(buf, n):
        def body(i, carry):
            send(buf.at[k, z], buf.at[k, z], many_send.at[n], many_recv.at[n], row=row_of(z + i, k))
            return carry

        lax.fori_loop(1, Z, body, 0)

    def z_to_sib(buf, n):
        got(buf.at[0, pl.ds(0, Z - 1)], many_recv.at[n])
        send(buf.at[k], buf.at[k], many_send.at[n + 1], many_recv.at[n + 1], row=row_of(z, 1 - k))

    z_step(1)
    sib_step(0)
    x_first()

    def student_logits():
        got(spt.at[1 - k], many_recv.at[2])
        part = jnp.zeros((PB, 128), F32)
        order = [PR * (2 * zz + kk) + u for kk in range(2) for zz in range(Z) for u in range(PR)]
        rhs = jnp.concatenate([sqx[i] for i in order], axis=0).astype(BF)
        unit = (pa == pb).astype(BF)
        for g in range(3):
            wide = spt[:, :, 8 * PR * g : 8 * PR * (g + 1), :].reshape(2 * Z * 8 * PR, PB)
            back = nt(unit, wide).astype(BF)
            part = jnp.where(lane_group == g, nn(back, rhs), part)
        sbuf[...] = SCALE * spread(part)

    p_index = c * PB + natural(rows_p)

    def onehot():
        wanted = jnp.zeros((1, 128), jnp.int32)
        within = lax.rem(lane, QB)
        for i in range(QB):
            wanted = jnp.where(within == i, pos_ref[i], wanted)
        return p_index == wanted

    def student_stats():
        s = sbuf[...]
        top = jnp.max(s, axis=0, keepdims=True)
        mass = jnp.sum(jnp.exp(s - top), axis=0, keepdims=True)
        hit = jnp.sum(jnp.where(onehot(), s, 0.0), axis=0, keepdims=True)
        sst[c] = jnp.where(lane_group == 0, top, jnp.where(lane_group == 1, mass, hit))
        to_col(lambda peer: sst.at[c], sst.at[c], 3)
        to_row(lambda peer: sqx.at[pl.ds(PR * peer, PR)], sqr.at[r], 4)
        sqr[r] = sqx[pl.ds(PR * r, PR)]

    def only(v, g):
        return spread(jnp.where(lane_group == g, v, 0.0))

    def pack(dst, weights, stats):
        hi, lo = split2(weights)
        table = spt[...].reshape(2 * Z * DR, PB)
        u = nn(jnp.concatenate([table, table], axis=1), jnp.concatenate([hi, lo], axis=0))
        for kk in range(2):
            for zz in range(Z):
                for uu in range(PR):
                    base = (kk * Z + zz) * DR + 8 * uu
                    piece = stats
                    for g in range(3):
                        at = base + 8 * PR * g
                        piece = jnp.where(lane_group == g, u[at : at + 8], piece)
                    dst[PR * (2 * zz + kk) + uu] = piece

    def student_slopes():
        got(sst.at[pl.ds(0, C - 1)], many_recv.at[3])
        rows = [sst[i] for i in range(C)]
        top = only(functools.reduce(jnp.maximum, rows), 0)
        mass = jnp.zeros((1, 128), F32)
        hit = jnp.zeros((1, 128), F32)
        for v in rows:
            mass = mass + jnp.where(lane_group == 0, jnp.exp(jnp.minimum(v - top, 0.0)) * pltpu.roll(v, 96, 1), 0.0)
            hit = hit + v
        mass = spread(mass)
        hit = only(hit, 2)
        zz_ = 2.0 * (jnp.exp(sbuf[...] - top) / mass) - jnp.where(onehot(), 1.0, 0.0)
        pack(upz, zz_, jnp.zeros((8, 128), F32))
        vbuf[c] = upz[c]
        quarter = PB // GROUPS
        small = jnp.zeros((quarter, 128), F32)
        for g in range(GROUPS):
            small = jnp.where(lane_group == g, zz_[quarter * g : quarter * (g + 1)], small)
        zag[k, z] = small
        to_z(zag, 6)
        return top + jnp.log(mass), hit

    def unpack_slopes():
        got(zag.at[1 - k], many_recv.at[7])
        quarter = PB // GROUPS
        for t in range(T):
            for g in range(GROUPS):
                tile = jnp.zeros((quarter, 128), F32)
                for b in range(GROUPS):
                    rr = GROUPS * t + b
                    v = zag[rr % 2, rr // 2]
                    if b != g:
                        v = pltpu.roll(v, ((b - g) % GROUPS) * QB, 1)
                    tile = jnp.where(lane_group == b, v, tile)
                zfull[t, quarter * g : quarter * (g + 1)] = tile

    def unpack_queries():
        got(sqr.at[pl.ds(0, R - 1)], many_recv.at[4])
        tiles = []
        for t in range(T):
            rows = []
            for u in range(PR):
                for g in range(3):
                    tile = jnp.zeros((8, 128), F32)
                    for b in range(GROUPS):
                        v = sqr[GROUPS * t + b, u]
                        if b != g:
                            v = pltpu.roll(v, ((b - g) % GROUPS) * QB, 1)
                        tile = jnp.where(lane_group == b, v, tile)
                    rows.append(tile)
            tiles.append(jnp.concatenate(rows, axis=0).astype(BF))
        return tiles

    half = Z // 2

    def at(s, kk):
        return [row_of(z + o, kk) for o in offsets if abs(o) == s]

    def numbers(s):
        return [j for j, o in enumerate(offsets) if abs(o) == s]

    def z_turn(s):
        z_got(s)
        if s < half:
            z_step(s + 1)
        for j in numbers(s):
            xy_step(j)

    def whole(s):
        for j in numbers(s):
            xy_got(j)
            sib_step(j + 1)

    def handed(s):
        for j in numbers(s):
            sib_got(j + 1)

    student = [x_second, x_last_and_y, *[functools.partial(y_turn, t) for t in range(1, YC // 2 + 1)]]

    def relay():
        if student:
            student.pop(0)()

    def spt_to_sib():
        send(spt.at[k], spt.at[k], many_send.at[2], many_recv.at[2], row=row_of(z, 1 - k))

    def logits():
        while student:
            relay()
        student_logits()
        student_stats()

    teach([sib_got(0)])
    z_turn(1)
    relay()
    if half >= 2:
        z_turn(2)
        relay()
    whole(1)
    if half >= 2:
        teach(at(1, k))
        relay()
        if half >= 3:
            z_turn(3)
        for s in range(2, half + 1):
            whole(s)
            if s + 2 <= half:
                z_turn(s + 2)
            if s + 2 == max(half, 4):
                spt_to_sib()
            if s < half:
                teach(at(s, k))
                relay()
                handed(s)
                teach(at(s, 1 - k))
                relay()
            else:
                logits()
                handed(s)
                teach(at(s, k) + at(s, 1 - k))
        handed(1)
        teach(at(1, 1 - k))
    else:
        spt_to_sib()
        logits()
        handed(1)
        teach(at(1, k) + at(1, 1 - k))

    for t in range(T):
        tile = tblk[GROUPS * t]
        for b in range(1, GROUPS):
            tile = jnp.where(lane_group == b, tblk[GROUPS * t + b], tile)
        tag[k, z, t] = tile
    to_z(tag, 8)
    student_lse, hit = student_slopes()
    got(tblk.at[pl.ds(0, R - 1)], many_recv.at[12])
    t_own = town[...].reshape(PB, 128)
    top = jnp.max(t_own, axis=0, keepdims=True)
    e = jnp.exp(t_own - top)
    mass = jnp.sum(e, axis=0, keepdims=True)
    cross = jnp.sum(e * (t_own - sbuf[...]), axis=0, keepdims=True)
    row8 = lax.broadcasted_iota(jnp.int32, (8, 128), 0)
    pack(upt, e, jnp.where(row8 == 0, top, jnp.where(row8 == 1, mass, cross)))
    ubuf[c] = upt[c]
    to_col(lambda peer: upt.at[peer], ubuf.at[c], 10)
    to_col(lambda peer: upz.at[peer], vbuf.at[c], 5)
    z_to_sib(zag, 6)
    sq_tiles = unpack_queries()
    got(ubuf.at[pl.ds(0, C - 1)], many_recv.at[10])
    tops = only(jnp.concatenate([ubuf[i, 0:1] for i in range(C)], axis=0), 3)
    top = jnp.max(tops, axis=0, keepdims=True)
    weights = jnp.exp(tops - top)
    acc = jnp.zeros((8, 128), F32)
    for i in range(C):
        acc = acc + weights[i : i + 1] * ubuf[i]
    whole = only(acc, 3)
    mass, cross = whole[1:2], whole[2:3]
    inverse = 1.0 / mass
    per_query = cross * inverse - (top + jnp.log(mass)) + 2.0 * student_lse - hit
    fin[r] = jnp.where(lane_group == 0, top, jnp.where(lane_group == 1, inverse, per_query))
    to_row(lambda peer: fin.at[r], fin.at[r], 11)
    z_to_sib(tag, 8)
    unpack_slopes()
    got(vbuf.at[pl.ds(0, C - 1)], many_recv.at[5])
    v_sum = functools.reduce(jnp.add, [vbuf[i] for i in range(C)])
    grads = (SCALE / total) * (v_sum - acc * inverse)
    for g in range(3):
        qg_ref[8 * g : 8 * g + 8, :] = (pltpu.roll(grads, 128 - QB * g, 1) if g else grads)[:, 0:QB]
    got(tag.at[1 - k], many_recv.at[9])

    got(fin.at[pl.ds(0, R - 1)], many_recv.at[11])
    grads = jnp.zeros((DR, PB), F32)
    per_query = jnp.zeros((1, 128), F32)
    for t in range(T):
        tops = jnp.zeros((1, 128), F32)
        inverses = jnp.zeros((1, 128), F32)
        for b in range(GROUPS):
            v = fin[GROUPS * t + b]
            per_query = per_query + jnp.where(lane_group == 2, v, 0.0)
            tops = jnp.where(lane_group == b, pltpu.roll(v, b * QB, 1) if b else v, tops)
            inverses = jnp.where(lane_group == b, pltpu.roll(v, ((b - 1) % GROUPS) * QB, 1) if b != 1 else v, inverses)
        slopes = zfull[t] - jnp.exp(tag[:, :, t].reshape(PB, 128) - tops) * inverses
        slopes = jnp.concatenate(
            [slopes[8 * (kk * Z + zz) : 8 * (kk * Z + zz) + 8] for zz in range(Z) for kk in range(2)], axis=0
        )
        hi, lo = split2(slopes)
        grads = grads + nt(jnp.concatenate([sq_tiles[t]] * 2, axis=1), jnp.concatenate([hi, lo], axis=1))
    pg_ref[...] = grads * (SCALE / total)
    loss_ref[...] = jnp.zeros((1, 1), F32) + jnp.sum(per_query) / total

    for s in range(1, Z // 2 + 1):
        last = s == Z // 2
        a, b = (mine_a, mine_b) if last else (mine, mine)
        left(qbuf.at[row_of(z - (s - 1), k), a], z_send.at[0, s - 1])
        left(qbuf.at[row_of(z + (s - 1), k), b], z_send.at[1, s - 1])
    for j in range(len(offsets)):
        b = row_of(z + offsets[j], k)
        for n, part in enumerate((mine, mine, mine_a, mine_b)):
            left(qbuf.at[b, part], xy_send.at[n, j])
    for j in range(len(offsets) + 1):
        left(qbuf.at[r], sib_send.at[j])
    for s in range(1, Z // 2 + 1):
        left(spt.at[k, z], s_send.at[0, s - 1])
        if s < Z // 2:
            left(spt.at[k, z], s_send.at[1, s - 1])
    for n in range(3):
        left(sqx.at[c], x_send.at[n])
    for s in range(1, YC // 2 + 1):
        left(chips(y), y_send.at[0, s - 1])
        if s < YC // 2:
            left(chips(y), y_send.at[1, s - 1])
    left(spt.at[k], many_send.at[2])
    for n, buf, count in ((3, sst, C), (5, upz, C), (10, upt, C), (4, sqr, R), (11, fin, R), (12, tblk, R)):
        left(buf.at[pl.ds(0, count - 1)], many_send.at[n])
    for n, buf in ((6, zag), (8, tag)):
        left(buf.at[0, pl.ds(0, Z - 1)], many_send.at[n])
        left(buf.at[0], many_send.at[n + 1])


def shards(query_tokens, query_lengths, passage_tokens, passage_lengths, student_queries, student_passages, positives):
    R = lax.axis_size("row")
    C = lax.axis_size("col")
    Z = R // 2
    L = query_tokens.shape[1]
    LP = passage_tokens.shape[1]
    PB = 8 * R
    PR = C // R
    DR = student_passages.shape[1]
    T = R // GROUPS
    hops = Z - 1
    YC = C // min(X_CHIPS, C)
    dma = pltpu.SemaphoreType.DMA
    vmem = pl.BlockSpec(memory_space=pltpu.VMEM)
    hbm = pl.BlockSpec(memory_space=pltpu.HBM)
    pg, qg, loss = pl.pallas_call(
        functools.partial(kernel, R, C),
        out_shape=(
            jax.ShapeDtypeStruct((DR, PB), F32),
            jax.ShapeDtypeStruct((24, QB), F32),
            jax.ShapeDtypeStruct((1, 1), F32),
        ),
        in_specs=[hbm] * 7,
        out_specs=(vmem, vmem, vmem),
        scratch_shapes=[
            pltpu.SMEM((QB,), jnp.int32),
            pltpu.SMEM((8,), jnp.int32),
            pltpu.SMEM((QB,), jnp.int32),
            pltpu.VMEM((24, QB), BF),
            pltpu.VMEM((DR, PB), BF),
            pltpu.VMEM((QB, L, 128), BF),
            pltpu.VMEM((8, LP, 128), BF),
            pltpu.VMEM((R, QB * L, 128), BF),
            pltpu.VMEM((LP * 8, 128), BF),
            pltpu.VMEM((C, 8, 128), F32),
            pltpu.VMEM((2, Z, DR, PB), BF),
            pltpu.VMEM((C, 1, 128), F32),
            pltpu.VMEM((PB, 128), F32),
            pltpu.VMEM((C, 8, 128), F32),
            pltpu.VMEM((C, 8, 128), F32),
            pltpu.VMEM((2, Z, PB // GROUPS, 128), F32),
            pltpu.VMEM((T, PB, 128), F32),
            pltpu.VMEM((R, PR, 8, 128), F32),
            pltpu.VMEM((R, 8, 128), F32),
            pltpu.VMEM((2, Z, 8, 128), F32),
            pltpu.VMEM((2, Z, T, 8, 128), F32),
            pltpu.VMEM((C, 8, 128), F32),
            pltpu.VMEM((C, 8, 128), F32),
            pltpu.VMEM((R, 1, 128), F32),
            dma((7,)),
            dma((2, Z // 2)),
            dma((2, Z // 2)),
            dma((2, Z // 2)),
            dma((2, Z // 2)),
            dma((3,)),
            dma((3,)),
            dma((2, YC // 2)),
            dma((2, YC // 2)),
            dma((4, hops)),
            dma((4, hops)),
            dma((hops + 1,)),
            dma((hops + 1,)),
            dma((13,)),
            dma((13,)),
        ],
        compiler_params=pltpu.CompilerParams(
            collective_id=0, has_side_effects=True, vmem_limit_bytes=64 * 1024 * 1024
        ),
        name="distill",
    )(query_tokens, query_lengths, passage_tokens, passage_lengths, student_queries.T, student_passages.T, positives)
    return qg.T, pg.T, loss.reshape(())


def solution(mesh):
    return jax.shard_map(
        shards,
        mesh=mesh,
        in_specs=(
            P("row", None, None),
            P("row"),
            P(("col", "row"), None, None),
            P(("col", "row")),
            P("row", "col"),
            P("col", "row"),
            P("row"),
        ),
        out_specs=(P("row", "col"), P("col", "row"), P()),
        check_vma=False,
    )
```

```python
import functools

import jax
import jax.numpy as jnp
from jax import lax
from jax.experimental import pallas as pl
from jax.experimental.pallas import tpu as pltpu
from jax.sharding import PartitionSpec as P

MESH = pl.DeviceIdType.MESH
SCALE = 4.0
X_CHIPS = 4
QB = 32
GROUPS = 128 // QB
BF = jnp.bfloat16
F32 = jnp.float32


def nt(a, b):
    return lax.dot_general(a, b, (((1,), (1,)), ((), ())), preferred_element_type=F32)


def nn(a, b):
    return lax.dot_general(a, b, (((1,), (0,)), ((), ())), preferred_element_type=F32)


def split2(v):
    hi = v.astype(BF)
    return hi, (v - hi.astype(F32)).astype(BF)


def spread(v):
    v = v + pltpu.roll(v, 64, 1)
    return v + pltpu.roll(v, 32, 1)


def kernel(
    R,
    C,
    qt_hbm,
    qlen_hbm,
    pt_hbm,
    plen_hbm,
    sq_hbm,
    sp_hbm,
    pos_hbm,
    pg_ref,
    qg_ref,
    loss_ref,
    qlen_ref,
    plen_ref,
    pos_ref,
    sq_ref,
    sp_ref,
    qraw,
    praw,
    qbuf,
    xbuf,
    sqx,
    spt,
    sst,
    sbuf,
    upz,
    vbuf,
    zag,
    zfull,
    sqr,
    tblk,
    town,
    tag,
    upt,
    ubuf,
    tst,
    sfin,
    fin,
    in_sem,
    near_sem,
    far_sem,
    z_send,
    z_recv,
    xy_send,
    xy_recv,
    sib_send,
    sib_recv,
    many_send,
    many_recv,
):
    Z = R // 2
    XC = min(X_CHIPS, C)
    YC = C // XC
    L = qt_hbm.shape[1]
    LP = pt_hbm.shape[1]
    N = QB * L
    SL = N // 4
    HALF = SL // 2
    PB = 8 * R
    PR = C // R
    DR = 24 * PR
    T = R // GROUPS
    total = QB * R

    r = lax.axis_index("row")
    c = lax.axis_index("col")
    z = lax.div(r, 2)
    k = lax.rem(r, 2)
    x = lax.rem(c, XC)
    y = lax.div(c, XC)
    color = lax.rem(jnp.where(k == 0, x + 2 * y, 2 * x + y), 4)

    def row_of(zz, kk):
        return lax.rem(zz + 2 * Z, Z) * 2 + kk

    def col_of(xx, yy):
        return lax.rem(yy + YC, YC) * XC + lax.rem(xx + XC, XC)

    def send(src, dst, s_sem, r_sem, **where):
        pltpu.make_async_remote_copy(
            src_ref=src, dst_ref=dst, send_sem=s_sem, recv_sem=r_sem, device_id=where, device_id_type=MESH
        ).start()

    def got(dst, r_sem):
        pltpu.make_async_remote_copy(
            src_ref=dst, dst_ref=dst, send_sem=r_sem, recv_sem=r_sem, device_id={"row": r}, device_id_type=MESH
        ).wait_recv()

    def left(src, s_sem):
        pltpu.make_async_remote_copy(
            src_ref=src, dst_ref=src, send_sem=s_sem, recv_sem=s_sem, device_id={"row": r}, device_id_type=MESH
        ).wait_send()

    barrier = pltpu.get_barrier_semaphore()

    def row_rank(rr):
        return lax.div(rr, 2) * 2 + 1 - lax.rem(rr, 2)

    def col_rank(cc):
        yy = lax.div(cc, XC)
        return jnp.where(yy < YC // 2, yy, YC // 2 + YC - 1 - yy) * XC + lax.rem(cc, XC)

    row_place, col_place = row_rank(r), col_rank(c)
    edges = (
        ({"row": row_of(z, 1 - k)}, row_rank(row_of(z, 1 - k)) > row_place, 0),
        ({"row": row_of(z + 1, k)}, row_rank(row_of(z + 1, k)) > row_place, 2),
        ({"row": row_of(z - 1, k)}, row_rank(row_of(z - 1, k)) > row_place, 1),
        ({"col": col_of(x + 1, y)}, col_rank(col_of(x + 1, y)) > col_place, 4),
        ({"col": col_of(x - 1, y)}, col_rank(col_of(x - 1, y)) > col_place, 3),
        ({"col": col_of(x, y + 1)}, col_rank(col_of(x, y + 1)) > col_place, 6),
        ({"col": col_of(x, y - 1)}, col_rank(col_of(x, y - 1)) > col_place, 5),
    )

    def row_at(place):
        return lax.div(place, 2) * 2 + 1 - lax.rem(place, 2)

    def col_at(place):
        yy = lax.div(place, XC)
        return jnp.where(yy < YC // 2, yy, YC // 2 + YC - 1 - yy) * XC + lax.rem(place, XC)

    def greet(sem, row_places, col_places):
        def rows(i, carry):
            pl.semaphore_signal(sem, inc=1, device_id={"row": row_at(i)}, device_id_type=MESH)
            return carry

        def cols(i, carry):
            pl.semaphore_signal(sem, inc=1, device_id={"col": col_at(i)}, device_id_type=MESH)
            return carry

        lax.fori_loop(*row_places, rows, 0)
        lax.fori_loop(*col_places, cols, 0)

    def edge(n):
        @pl.when(edges[n][1])
        def _():
            pl.semaphore_wait(near_sem.at[n], 1)

    inputs = [
        pltpu.make_async_copy(src, dst, in_sem.at[n])
        for n, (src, dst) in enumerate(
            (
                (qt_hbm, qraw),
                (qlen_hbm, qlen_ref),
                (pt_hbm, praw),
                (plen_hbm, plen_ref),
                (sq_hbm, sq_ref),
                (sp_hbm, sp_ref),
                (pos_hbm, pos_ref),
            )
        )
    ]
    for copy in inputs:
        copy.start()
    greet(barrier, (row_place + 1, R), (col_place + 1, C))

    rows_p = lax.broadcasted_iota(jnp.int32, (PB, 128), 0)
    lane = lax.broadcasted_iota(jnp.int32, (1, 128), 1)
    lane_group = lax.div(lane, QB)

    def natural(i):
        rank = lax.div(i, 8)
        return (2 * lax.rem(rank, Z) + lax.div(rank, Z)) * 8 + lax.rem(i, 8)

    inputs[0].wait()
    inputs[1].wait()
    slot = lax.broadcasted_iota(jnp.int32, (L, 128), 0)
    q32 = jnp.stack(
        [jnp.where(slot < qlen_ref[i], qraw[i].astype(F32), 0.0) for i in range(QB)], axis=0
    )
    qbuf[r] = jnp.swapaxes(q32, 0, 1).reshape(N, 128).astype(BF)


    inputs[4].wait()
    inputs[5].wait()
    qa = lax.broadcasted_iota(jnp.int32, (QB, 128), 0)
    qb = lax.broadcasted_iota(jnp.int32, (QB, 128), 1)
    sq_wide = nn(sq_ref[...], (qa == lax.rem(qb, QB)).astype(BF))
    packed = jnp.zeros((8, 128), F32)
    for g in range(3):
        packed = jnp.where(lane_group == g, sq_wide[8 * g : 8 * g + 8], packed)
    sqx[c] = packed
    pa = lax.broadcasted_iota(jnp.int32, (PB, PB), 0)
    pb = lax.broadcasted_iota(jnp.int32, (PB, PB), 1)
    sp_wide = nn(sp_ref[...], (pa == natural(pb)).astype(BF))
    spt[k, z] = jnp.concatenate(
        [sp_wide[24 * u + 8 * g : 24 * u + 8 * g + 8] for g in range(3) for u in range(PR)], axis=0
    ).astype(BF)

    inputs[2].wait()
    inputs[3].wait()
    inputs[6].wait()
    pslot = lax.broadcasted_iota(jnp.int32, (LP, 128), 0)
    p32 = []
    for i in range(8):
        rows = praw[i].astype(F32)
        p32.append(jnp.where(pslot < plen_ref[i], rows, rows[0:1]))
    xbuf[...] = jnp.swapaxes(jnp.stack(p32, axis=0), 0, 1).reshape(LP * 8, 128).astype(BF)

    def maxsim(b):
        s = nt(xbuf[...], qbuf[b])
        m = jnp.max(s.reshape(LP, 8, N), axis=0)
        acc = m[:, 0:128]
        for t in range(1, N // 128):
            acc = acc + m[:, 128 * t : 128 * t + 128]
        return spread(acc)

    def teach(blocks):
        found = [maxsim(b) for b in blocks]
        for b, v in zip(blocks, found):
            tblk[b] = v
        for b in blocks:
            send(tblk.at[b], town.at[k, z], many_send.at[12], many_recv.at[12], row=b)

    own = maxsim(r)
    tblk[r] = own
    town[k, z] = own

    @pl.when(row_place + col_place > 0)
    def _():
        pl.semaphore_wait(barrier, row_place + col_place)

    for peer, later, back in edges:

        @pl.when(jnp.logical_not(later))
        def _(peer=peer, back=back):
            pl.semaphore_signal(near_sem.at[back], inc=1, device_id=peer, device_id_type=MESH)


    mine = pl.ds(pl.multiple_of(color * SL, SL), SL)
    mine_a = pl.ds(pl.multiple_of(color * SL, HALF), HALF)
    mine_b = pl.ds(pl.multiple_of(color * SL + HALF, HALF), HALF)

    half = Z // 2
    ways = (jnp.where(z < 2, 1, 0), jnp.where(z < 2, 0, 1))
    levels = [[(w, s) for w in ways] for s in range(1, half)] + [[(0, half)]]
    numbers = [[2 * n + w for w in range(len(level))] for n, level in enumerate(levels)]

    def block(way, s, kk):
        return row_of(z + (2 * way - 1) * s, kk)

    blocks = [(way, s) for level in levels for way, s in level]

    def z_step(way, s):
        b = block(way, s - 1, k)
        send(
            qbuf.at[b, mine], qbuf.at[b, mine], z_send.at[way, s - 1], z_recv.at[way, s - 1], row=row_of(z + 1 - 2 * way, k)
        )

    def z_got(way, s):
        got(qbuf.at[block(way, s, k), mine], z_recv.at[way, s - 1])

    def xy_regions():
        one = lax.rem(color + 3, 4) * SL
        two = lax.rem(color + 1, 4) * SL
        far = lax.rem(color + 2, 4) * SL
        return (
            pl.ds(pl.multiple_of(one, SL), SL),
            pl.ds(pl.multiple_of(two, SL), SL),
            pl.ds(pl.multiple_of(far, HALF), HALF),
            pl.ds(pl.multiple_of(far + HALF, HALF), HALF),
        )

    def xy_step(j):
        b = block(*blocks[j], k)
        beside = (col_of(x + 1, y), col_of(x - 1, y))
        above = (col_of(x, y + 1), col_of(x, y - 1))
        to = [jnp.where(k == 0, a, b) for a, b in zip(beside + above, above + beside)]
        for n, (part, peer) in enumerate(zip((mine, mine, mine_a, mine_b), to)):
            send(qbuf.at[b, part], qbuf.at[b, part], xy_send.at[n, j], xy_recv.at[n, j], col=peer)

    def xy_got(j):
        b = block(*blocks[j], k)
        for n, part in enumerate(xy_regions()):
            got(qbuf.at[b, part], xy_recv.at[n, j])

    def sib_step(j):
        b = r if j == 0 else block(*blocks[j - 1], k)
        send(qbuf.at[b], qbuf.at[b], sib_send.at[j], sib_recv.at[j], row=row_of(z, 1 - k))

    def sib_got(j):
        b = row_of(z, 1 - k) if j == 0 else block(*blocks[j - 1], 1 - k)
        got(qbuf.at[b], sib_recv.at[j])
        return b

    def to_col(src_of, dst, n):
        def body(i, carry):
            peer = lax.rem(c + i, C)
            send(src_of(peer), dst, many_send.at[n], many_recv.at[n], col=peer)
            return carry

        lax.fori_loop(1, C, body, 0)

    def to_row(src_of, dst, n):
        def body(i, carry):
            peer = lax.rem(r + i, R)
            send(src_of(peer), dst, many_send.at[n], many_recv.at[n], row=peer)
            return carry

        lax.fori_loop(1, R, body, 0)

    def to_z(buf, n):
        def body(i, carry):
            send(buf.at[k, z], buf.at[k, z], many_send.at[n], many_recv.at[n], row=row_of(z + i, k))
            return carry

        lax.fori_loop(1, Z, body, 0)

    def z_to_sib(buf, n, m):
        got(buf.at[0, pl.ds(0, Z - 1)], many_recv.at[n])
        send(buf.at[k], buf.at[k], many_send.at[m], many_recv.at[m], row=row_of(z, 1 - k))

    edge(0)
    sib_step(0)
    lead = jnp.where(z == 0, 0, 1)
    for way in (lead, 1 - lead):

        @pl.when(jnp.where(way == 0, edges[1][1], edges[2][1]))
        def _(way=way):
            pl.semaphore_wait(near_sem.at[1 + way], 1)

        z_step(way, 1)
    greet(far_sem, (0, row_place), (0, col_place))

    def student_logits():
        got(sqx.at[pl.ds(0, C - 1)], many_recv.at[0])
        got(spt.at[1 - k], many_recv.at[14])
        part = jnp.zeros((PB, 128), F32)
        order = [PR * (2 * zz + kk) + u for kk in range(2) for zz in range(Z) for u in range(PR)]
        rhs = jnp.concatenate([sqx[i] for i in order], axis=0).astype(BF)
        unit = (pa == pb).astype(BF)
        for g in range(3):
            wide = spt[:, :, 8 * PR * g : 8 * PR * (g + 1), :].reshape(2 * Z * 8 * PR, PB)
            back = nt(unit, wide).astype(BF)
            part = jnp.where(lane_group == g, nn(back, rhs), part)
        s = SCALE * spread(part)
        sbuf[...] = s
        quarter = PB // GROUPS
        small = jnp.zeros((quarter, 128), F32)
        for g in range(GROUPS):
            small = jnp.where(lane_group == g, s[quarter * g : quarter * (g + 1)], small)
        zag[k, z] = small
        to_z(zag, 6)

    p_index = c * PB + natural(rows_p)

    def onehot():
        wanted = jnp.zeros((1, 128), jnp.int32)
        within = lax.rem(lane, QB)
        for i in range(QB):
            wanted = jnp.where(within == i, pos_ref[i], wanted)
        return p_index == wanted

    def student_stats():
        s = sbuf[...]
        top = jnp.max(s, axis=0, keepdims=True)
        mass = jnp.sum(jnp.exp(s - top), axis=0, keepdims=True)
        hit = jnp.sum(jnp.where(onehot(), s, 0.0), axis=0, keepdims=True)
        sst[c] = jnp.where(lane_group == 0, top, jnp.where(lane_group == 1, mass, hit))
        to_col(lambda peer: sst.at[c], sst.at[c], 3)
        to_row(lambda peer: sqx.at[pl.ds(PR * peer, PR)], sqr.at[r], 4)
        sqr[r] = sqx[pl.ds(PR * r, PR)]

    def only(v, g):
        return spread(jnp.where(lane_group == g, v, 0.0))

    def pack(dst, weights):
        hi, lo = split2(weights)
        table = spt[...].reshape(2 * Z * DR, PB)
        u = nn(jnp.concatenate([table, table], axis=1), jnp.concatenate([hi, lo], axis=0))
        for kk in range(2):
            for zz in range(Z):
                for uu in range(PR):
                    base = (kk * Z + zz) * DR + 8 * uu
                    piece = jnp.zeros((8, 128), F32)
                    for g in range(3):
                        at = base + 8 * PR * g
                        piece = jnp.where(lane_group == g, u[at : at + 8], piece)
                    dst[PR * (2 * zz + kk) + uu] = piece

    def softmax_parts(buf):
        rows = jnp.concatenate([buf[i] for i in range(C)], axis=0)
        tops = only(rows, 0)
        top = jnp.max(tops, axis=0, keepdims=True)
        weights = jnp.exp(tops - top)
        mass = only(jnp.sum(jnp.where(lane_group == 1, weights * rows, 0.0), axis=0, keepdims=True), 1)
        return top, mass, only(jnp.sum(rows, axis=0, keepdims=True), 2), weights

    def student_slopes():
        got(sst.at[pl.ds(0, C - 1)], many_recv.at[3])
        top, mass, hit, _ = softmax_parts(sst)
        zz_ = 2.0 * (jnp.exp(sbuf[...] - top) / mass) - jnp.where(onehot(), 1.0, 0.0)
        pack(upz, zz_)
        vbuf[c] = upz[c]
        to_col(lambda peer: upz.at[peer], vbuf.at[c], 5)
        wanted = jnp.zeros((1, 128), F32)
        within = lax.rem(lane, QB)
        for i in range(QB):
            wanted = jnp.where(within == i, pos_ref[i].astype(F32), wanted)
        sfin[r] = jnp.where(lane_group == 0, top, jnp.where(lane_group == 1, 1.0 / mass, wanted))
        to_row(lambda peer: sfin.at[r], sfin.at[r], 2)
        return top + jnp.log(mass), hit

    def row_vector(buf, t, g):
        tile = jnp.zeros((1, 128), F32)
        for b in range(GROUPS):
            v = buf[GROUPS * t + b]
            tile = jnp.where(lane_group == b, pltpu.roll(v, ((b - g) % GROUPS) * QB, 1) if b != g else v, tile)
        return tile

    def unpack_slopes():
        got(zag.at[1 - k], many_recv.at[7])
        got(sfin.at[pl.ds(0, R - 1)], many_recv.at[2])
        quarter = PB // GROUPS
        places = p_index.astype(F32)
        for t in range(T):
            for g in range(GROUPS):
                tile = jnp.zeros((quarter, 128), F32)
                for b in range(GROUPS):
                    rr = GROUPS * t + b
                    v = zag[rr % 2, rr // 2]
                    if b != g:
                        v = pltpu.roll(v, ((b - g) % GROUPS) * QB, 1)
                    tile = jnp.where(lane_group == b, v, tile)
                zfull[t, quarter * g : quarter * (g + 1)] = tile
            probs = jnp.exp(zfull[t] - row_vector(sfin, t, 0)) * row_vector(sfin, t, 1)
            zfull[t] = 2.0 * probs - jnp.where(places == row_vector(sfin, t, 2), 1.0, 0.0)

    def unpack_queries():
        got(sqr.at[pl.ds(0, R - 1)], many_recv.at[4])
        tiles = []
        for t in range(T):
            rows = []
            for u in range(PR):
                for g in range(3):
                    tile = jnp.zeros((8, 128), F32)
                    for b in range(GROUPS):
                        v = sqr[GROUPS * t + b, u]
                        if b != g:
                            v = pltpu.roll(v, ((b - g) % GROUPS) * QB, 1)
                        tile = jnp.where(lane_group == b, v, tile)
                    rows.append(tile)
            tiles.append(jnp.concatenate(rows, axis=0).astype(BF))
        return tiles

    def turn(n):
        for (way, s), number in zip(levels[n], numbers[n]):
            z_got(way, s)
            if s < half - 1:
                z_step(way, s + 1)
            if n == 0 and number == 0:
                for e in (3, 4, 5, 6):
                    edge(e)
            xy_step(number)
        if n == half - 2:
            z_step(0, half)

    def whole(n):
        for number in numbers[n]:
            xy_got(number)
            sib_step(number + 1)

    def handed(n):
        for number in numbers[n]:
            sib_got(number + 1)

    def at(n, kk):
        return [block(way, s, kk) for way, s in levels[n]]

    turn(0)
    teach([sib_got(0)])
    turn(1)
    whole(0)

    @pl.when(row_place + col_place < R + C - 2)
    def _():
        pl.semaphore_wait(far_sem, R - 1 - row_place + C - 1 - col_place)

    to_col(lambda peer: sqx.at[c], sqx.at[c], 0)
    to_z(spt, 1)
    teach(at(0, k))
    for n in range(1, half):
        if n + 1 < half:
            turn(n + 1)
        if n == half - 1:
            student_logits()
            student_stats()
        whole(n)
        if n < half - 1:
            teach(at(n, k))
            handed(n)
            teach(at(n, 1 - k))
        if n == max(half - 3, 1):
            z_to_sib(spt, 1, 14)
        if n == half - 1:
            handed(n)
            teach(at(n, k) + at(n, 1 - k))
    handed(0)
    teach(at(0, 1 - k))

    for t in range(T):
        tile = tblk[GROUPS * t]
        for b in range(1, GROUPS):
            tile = jnp.where(lane_group == b, tblk[GROUPS * t + b], tile)
        tag[k, z, t] = tile
    student_lse, hit = student_slopes()
    z_to_sib(zag, 6, 7)
    got(tblk.at[pl.ds(0, R - 1)], many_recv.at[12])
    t_own = town[...].reshape(PB, 128)
    top = jnp.max(t_own, axis=0, keepdims=True)
    e = jnp.exp(t_own - top)
    mass = jnp.sum(e, axis=0, keepdims=True)
    cross = jnp.sum(e * (t_own - sbuf[...]), axis=0, keepdims=True)
    tst[c] = jnp.where(lane_group == 0, top, jnp.where(lane_group == 1, mass, cross))
    to_col(lambda peer: tst.at[c], tst.at[c], 13)
    pack(upt, e)
    ubuf[c] = upt[c]
    to_col(lambda peer: upt.at[peer], ubuf.at[c], 10)
    to_z(tag, 8)
    sq_tiles = unpack_queries()
    got(vbuf.at[pl.ds(0, C - 1)], many_recv.at[5])
    v_sum = functools.reduce(jnp.add, [vbuf[i] for i in range(C)])
    unpack_slopes()

    got(tst.at[pl.ds(0, C - 1)], many_recv.at[13])
    top, mass, _, weights = softmax_parts(tst)
    rows = jnp.concatenate([tst[i] for i in range(C)], axis=0)
    cross = only(jnp.sum(weights * rows, axis=0, keepdims=True), 2)
    inverse = 1.0 / mass
    per_query = cross * inverse - (top + jnp.log(mass)) + 2.0 * student_lse - hit
    fin[r] = jnp.where(lane_group == 0, top, jnp.where(lane_group == 1, inverse, per_query))
    to_row(lambda peer: fin.at[r], fin.at[r], 11)
    z_to_sib(tag, 8, 9)
    got(ubuf.at[pl.ds(0, C - 1)], many_recv.at[10])
    acc = jnp.zeros((8, 128), F32)
    for i in range(C):
        acc = acc + weights[i : i + 1] * ubuf[i]
    grads = (SCALE / total) * (v_sum - acc * inverse)
    for g in range(3):
        qg_ref[8 * g : 8 * g + 8, :] = (pltpu.roll(grads, 128 - QB * g, 1) if g else grads)[:, 0:QB]
    got(tag.at[1 - k], many_recv.at[9])

    got(fin.at[pl.ds(0, R - 1)], many_recv.at[11])
    grads = jnp.zeros((DR, PB), F32)
    per_query = jnp.zeros((1, 128), F32)
    for t in range(T):
        tops = row_vector(fin, t, 0)
        inverses = row_vector(fin, t, 1)
        for b in range(GROUPS):
            per_query = per_query + jnp.where(lane_group == 2, fin[GROUPS * t + b], 0.0)
        slopes = zfull[t] - jnp.exp(tag[:, :, t].reshape(PB, 128) - tops) * inverses
        slopes = jnp.concatenate(
            [slopes[8 * (kk * Z + zz) : 8 * (kk * Z + zz) + 8] for zz in range(Z) for kk in range(2)], axis=0
        )
        hi, lo = split2(slopes)
        grads = grads + nt(jnp.concatenate([sq_tiles[t]] * 2, axis=1), jnp.concatenate([hi, lo], axis=1))
    pg_ref[...] = grads * (SCALE / total)
    loss_ref[...] = jnp.zeros((1, 1), F32) + jnp.sum(per_query) / total

    for s in range(1, half + 1):
        left(qbuf.at[r, mine], z_send.at[0, s - 1])
        if s < half:
            left(qbuf.at[r, mine], z_send.at[1, s - 1])
    for j in range(len(blocks)):
        for n, part in enumerate((mine, mine, mine_a, mine_b)):
            left(qbuf.at[r, part], xy_send.at[n, j])
    for j in range(len(blocks) + 1):
        left(qbuf.at[r], sib_send.at[j])
    for n, buf, count in ((0, sqx, C), (2, sfin, R), (13, tst, C), (3, sst, C), (5, upz, C), (10, upt, C), (4, sqr, R), (11, fin, R), (12, tblk, R)):
        left(buf.at[pl.ds(0, count - 1)], many_send.at[n])
    for n, m, buf in ((1, 14, spt), (6, 7, zag), (8, 9, tag)):
        left(buf.at[0, pl.ds(0, Z - 1)], many_send.at[n])
        left(buf.at[0], many_send.at[m])


def shards(query_tokens, query_lengths, passage_tokens, passage_lengths, student_queries, student_passages, positives):
    R = lax.axis_size("row")
    C = lax.axis_size("col")
    Z = R // 2
    L = query_tokens.shape[1]
    LP = passage_tokens.shape[1]
    PB = 8 * R
    PR = C // R
    DR = student_passages.shape[1]
    T = R // GROUPS
    hops = Z - 1
    dma = pltpu.SemaphoreType.DMA
    vmem = pl.BlockSpec(memory_space=pltpu.VMEM)
    hbm = pl.BlockSpec(memory_space=pltpu.HBM)
    pg, qg, loss = pl.pallas_call(
        functools.partial(kernel, R, C),
        out_shape=(
            jax.ShapeDtypeStruct((DR, PB), F32),
            jax.ShapeDtypeStruct((24, QB), F32),
            jax.ShapeDtypeStruct((1, 1), F32),
        ),
        in_specs=[hbm] * 7,
        out_specs=(vmem, vmem, vmem),
        scratch_shapes=[
            pltpu.SMEM((QB,), jnp.int32),
            pltpu.SMEM((8,), jnp.int32),
            pltpu.SMEM((QB,), jnp.int32),
            pltpu.VMEM((24, QB), BF),
            pltpu.VMEM((DR, PB), BF),
            pltpu.VMEM((QB, L, 128), BF),
            pltpu.VMEM((8, LP, 128), BF),
            pltpu.VMEM((R, QB * L, 128), BF),
            pltpu.VMEM((LP * 8, 128), BF),
            pltpu.VMEM((C, 8, 128), F32),
            pltpu.VMEM((2, Z, DR, PB), BF),
            pltpu.VMEM((C, 1, 128), F32),
            pltpu.VMEM((PB, 128), F32),
            pltpu.VMEM((C, 8, 128), F32),
            pltpu.VMEM((C, 8, 128), F32),
            pltpu.VMEM((2, Z, PB // GROUPS, 128), F32),
            pltpu.VMEM((T, PB, 128), F32),
            pltpu.VMEM((R, PR, 8, 128), F32),
            pltpu.VMEM((R, 8, 128), F32),
            pltpu.VMEM((2, Z, 8, 128), F32),
            pltpu.VMEM((2, Z, T, 8, 128), F32),
            pltpu.VMEM((C, 8, 128), F32),
            pltpu.VMEM((C, 8, 128), F32),
            pltpu.VMEM((C, 1, 128), F32),
            pltpu.VMEM((R, 1, 128), F32),
            pltpu.VMEM((R, 1, 128), F32),
            dma((7,)),
            pltpu.SemaphoreType.REGULAR((7,)),
            pltpu.SemaphoreType.REGULAR,
            dma((2, Z // 2)),
            dma((2, Z // 2)),
            dma((4, hops)),
            dma((4, hops)),
            dma((hops + 1,)),
            dma((hops + 1,)),
            dma((15,)),
            dma((15,)),
        ],
        compiler_params=pltpu.CompilerParams(
            collective_id=0, has_side_effects=True, vmem_limit_bytes=64 * 1024 * 1024
        ),
        name="distill",
    )(query_tokens, query_lengths, passage_tokens, passage_lengths, student_queries.T, student_passages.T, positives)
    return qg.T, pg.T, loss.reshape(())


def solution(mesh):
    return jax.shard_map(
        shards,
        mesh=mesh,
        in_specs=(
            P("row", None, None),
            P("row"),
            P(("col", "row"), None, None),
            P(("col", "row")),
            P("row", "col"),
            P("col", "row"),
            P("row"),
        ),
        out_specs=(P("row", "col"), P("col", "row"), P()),
        check_vma=False,
    )
```

```python
import functools

import jax
import jax.numpy as jnp
from jax import lax
from jax.experimental import pallas as pl
from jax.experimental.pallas import tpu as pltpu
from jax.sharding import PartitionSpec as P

MESH = pl.DeviceIdType.MESH
SCALE = 4.0
X_CHIPS = 4
QB = 32
GROUPS = 128 // QB
BF = jnp.bfloat16
F32 = jnp.float32


def nt(a, b):
    return lax.dot_general(a, b, (((1,), (1,)), ((), ())), preferred_element_type=F32)


def nn(a, b):
    return lax.dot_general(a, b, (((1,), (0,)), ((), ())), preferred_element_type=F32)


def split2(v):
    hi = v.astype(BF)
    return hi, (v - hi.astype(F32)).astype(BF)


def spread(v):
    v = v + pltpu.roll(v, 64, 1)
    return v + pltpu.roll(v, 32, 1)


def kernel(
    R,
    C,
    qt_hbm,
    qlen_hbm,
    pt_hbm,
    plen_hbm,
    sq_hbm,
    sp_hbm,
    pos_hbm,
    pg_ref,
    qg_ref,
    loss_ref,
    qlen_ref,
    plen_ref,
    pos_ref,
    wanted_ref,
    sq_ref,
    sp_ref,
    qraw,
    praw,
    qbuf,
    xbuf,
    sqx,
    spt,
    sst,
    sbuf,
    upz,
    vbuf,
    zag,
    zfull,
    sqr,
    tblk,
    town,
    tag,
    upt,
    ubuf,
    tst,
    sfin,
    fin,
    in_sem,
    near_sem,
    far_sem,
    z_send,
    z_recv,
    xy_send,
    xy_recv,
    sib_send,
    sib_recv,
    many_send,
    many_recv,
):
    Z = R // 2
    XC = min(X_CHIPS, C)
    YC = C // XC
    L = qt_hbm.shape[1]
    LP = pt_hbm.shape[1]
    N = QB * L
    SL = N // 4
    HALF = SL // 2
    PB = 8 * R
    PR = C // R
    DR = 24 * PR
    T = R // GROUPS
    total = QB * R

    r = lax.axis_index("row")
    c = lax.axis_index("col")
    z = lax.div(r, 2)
    k = lax.rem(r, 2)
    x = lax.rem(c, XC)
    y = lax.div(c, XC)
    color = lax.rem(jnp.where(k == 0, x + 2 * y, 2 * x + y), 4)

    def row_of(zz, kk):
        return lax.rem(zz + 2 * Z, Z) * 2 + kk

    def col_of(xx, yy):
        return lax.rem(yy + YC, YC) * XC + lax.rem(xx + XC, XC)

    def send(src, dst, s_sem, r_sem, **where):
        pltpu.make_async_remote_copy(
            src_ref=src, dst_ref=dst, send_sem=s_sem, recv_sem=r_sem, device_id=where, device_id_type=MESH
        ).start()

    def got(dst, r_sem):
        pltpu.make_async_remote_copy(
            src_ref=dst, dst_ref=dst, send_sem=r_sem, recv_sem=r_sem, device_id={"row": r}, device_id_type=MESH
        ).wait_recv()

    def left(src, s_sem):
        pltpu.make_async_remote_copy(
            src_ref=src, dst_ref=src, send_sem=s_sem, recv_sem=s_sem, device_id={"row": r}, device_id_type=MESH
        ).wait_send()

    barrier = pltpu.get_barrier_semaphore()

    def row_rank(rr):
        return lax.div(rr, 2) * 2 + 1 - lax.rem(rr, 2)

    def col_rank(cc):
        yy = lax.div(cc, XC)
        return jnp.where(yy < YC // 2, yy, YC // 2 + YC - 1 - yy) * XC + lax.rem(cc, XC)

    row_place, col_place = row_rank(r), col_rank(c)
    edges = (
        ({"row": row_of(z, 1 - k)}, row_rank(row_of(z, 1 - k)) > row_place, 0),
        ({"row": row_of(z + 1, k)}, row_rank(row_of(z + 1, k)) > row_place, 2),
        ({"row": row_of(z - 1, k)}, row_rank(row_of(z - 1, k)) > row_place, 1),
        ({"col": col_of(x + 1, y)}, col_rank(col_of(x + 1, y)) > col_place, 4),
        ({"col": col_of(x - 1, y)}, col_rank(col_of(x - 1, y)) > col_place, 3),
        ({"col": col_of(x, y + 1)}, col_rank(col_of(x, y + 1)) > col_place, 6),
        ({"col": col_of(x, y - 1)}, col_rank(col_of(x, y - 1)) > col_place, 5),
    )

    def row_at(place):
        return lax.div(place, 2) * 2 + 1 - lax.rem(place, 2)

    def col_at(place):
        yy = lax.div(place, XC)
        return jnp.where(yy < YC // 2, yy, YC // 2 + YC - 1 - yy) * XC + lax.rem(place, XC)

    def greet(sem, row_places, col_places):
        def rows(i, carry):
            pl.semaphore_signal(sem, inc=1, device_id={"row": row_at(i)}, device_id_type=MESH)
            return carry

        def cols(i, carry):
            pl.semaphore_signal(sem, inc=1, device_id={"col": col_at(i)}, device_id_type=MESH)
            return carry

        lax.fori_loop(*row_places, rows, 0)
        lax.fori_loop(*col_places, cols, 0)

    def edge(n):
        @pl.when(edges[n][1])
        def _():
            pl.semaphore_wait(near_sem.at[n], 1)

    inputs = [
        pltpu.make_async_copy(src, dst, in_sem.at[n])
        for n, (src, dst) in enumerate(
            (
                (qt_hbm, qraw),
                (qlen_hbm, qlen_ref),
                (pt_hbm, praw),
                (plen_hbm, plen_ref),
                (sq_hbm, sq_ref),
                (sp_hbm, sp_ref),
                (pos_hbm, pos_ref),
            )
        )
    ]
    for copy in inputs:
        copy.start()
    greet(barrier, (row_place + 1, R), (col_place + 1, C))

    rows_p = lax.broadcasted_iota(jnp.int32, (PB, 128), 0)
    lane = lax.broadcasted_iota(jnp.int32, (1, 128), 1)
    lane_group = lax.div(lane, QB)

    inputs[0].wait()
    inputs[1].wait()
    slot = lax.broadcasted_iota(jnp.int32, (L, 128), 0)
    q32 = jnp.stack(
        [jnp.where(slot < qlen_ref[i], qraw[i].astype(F32), 0.0) for i in range(QB)], axis=0
    )
    qbuf[z] = jnp.swapaxes(q32, 0, 1).reshape(N, 128).astype(BF)


    inputs[4].wait()
    inputs[5].wait()
    qa = lax.broadcasted_iota(jnp.int32, (QB, 128), 0)
    qb = lax.broadcasted_iota(jnp.int32, (QB, 128), 1)
    sq_wide = nn(sq_ref[...], (qa == lax.rem(qb, QB)).astype(BF))
    packed = jnp.zeros((8, 128), F32)
    for g in range(3):
        packed = jnp.where(lane_group == g, sq_wide[8 * g : 8 * g + 8], packed)
    sqx[c] = packed
    sp_wide = sp_ref[...].astype(F32)
    spt[k, z] = jnp.concatenate(
        [sp_wide[24 * u + 8 * g : 24 * u + 8 * g + 8] for g in range(3) for u in range(PR)], axis=0
    ).astype(BF)

    inputs[6].wait()
    wanted = jnp.zeros((1, 128), F32)
    within = lax.rem(lane, QB)
    for i in range(QB):
        wanted = jnp.where(within == i, pos_ref[i].astype(F32), wanted)
    wanted_ref[...] = wanted

    inputs[2].wait()
    inputs[3].wait()
    pslot = lax.broadcasted_iota(jnp.int32, (LP, 128), 0)
    p32 = []
    for i in range(8):
        rows = praw[i].astype(F32)
        p32.append(jnp.where(pslot < plen_ref[i], rows, rows[0:1]))
    xbuf[k] = jnp.swapaxes(jnp.stack(p32, axis=0), 0, 1).reshape(LP * 8, 128).astype(BF)

    def maxsim(tokens, zz):
        s = nt(tokens, qbuf[zz])
        m = jnp.max(s.reshape(-1, LP, 8, N), axis=1).reshape(-1, N)
        acc = m[:, 0:128]
        for t in range(1, N // 128):
            acc = acc + m[:, 128 * t : 128 * t + 128]
        return spread(acc)

    def teach(zz):
        tblk[zz] = maxsim(xbuf[...].reshape(2 * LP * 8, 128), zz).reshape(2, 8, 128)
        send(tblk.at[zz], town.at[z], many_send.at[12], many_recv.at[12], row=row_of(zz, k))

    tblk[z, k] = maxsim(xbuf[k], z)

    @pl.when(row_place + col_place > 0)
    def _():
        pl.semaphore_wait(barrier, row_place + col_place)

    for peer, later, back in edges:

        @pl.when(jnp.logical_not(later))
        def _(peer=peer, back=back):
            pl.semaphore_signal(near_sem.at[back], inc=1, device_id=peer, device_id_type=MESH)


    mine = pl.ds(pl.multiple_of(color * SL, SL), SL)
    mine_a = pl.ds(pl.multiple_of(color * SL, HALF), HALF)
    mine_b = pl.ds(pl.multiple_of(color * SL + HALF, HALF), HALF)

    half = Z // 2
    ways = (jnp.where(z < 2, 1, 0), jnp.where(z < 2, 0, 1))
    levels = [[(w, s) for w in ways] for s in range(1, half)] + [[(0, half)]]
    numbers = [[2 * n + w for w in range(len(level))] for n, level in enumerate(levels)]

    def block(way, s):
        return lax.rem(z + (2 * way - 1) * s + Z, Z)

    blocks = [(way, s) for level in levels for way, s in level]

    def z_step(way, s):
        b = block(way, s - 1)
        send(
            qbuf.at[b, mine], qbuf.at[b, mine], z_send.at[way, s - 1], z_recv.at[way, s - 1], row=row_of(z + 1 - 2 * way, k)
        )

    def z_got(way, s):
        got(qbuf.at[block(way, s), mine], z_recv.at[way, s - 1])

    def xy_regions():
        one = lax.rem(color + 3, 4) * SL
        two = lax.rem(color + 1, 4) * SL
        far = lax.rem(color + 2, 4) * SL
        return (
            pl.ds(pl.multiple_of(one, SL), SL),
            pl.ds(pl.multiple_of(two, SL), SL),
            pl.ds(pl.multiple_of(far, HALF), HALF),
            pl.ds(pl.multiple_of(far + HALF, HALF), HALF),
        )

    def xy_step(j):
        b = block(*blocks[j])
        beside = (col_of(x + 1, y), col_of(x - 1, y))
        above = (col_of(x, y + 1), col_of(x, y - 1))
        to = [jnp.where(k == 0, a, b) for a, b in zip(beside + above, above + beside)]
        for n, (part, peer) in enumerate(zip((mine, mine, mine_a, mine_b), to)):
            send(qbuf.at[b, part], qbuf.at[b, part], xy_send.at[n, j], xy_recv.at[n, j], col=peer)

    def xy_got(j):
        b = block(*blocks[j])
        for n, part in enumerate(xy_regions()):
            got(qbuf.at[b, part], xy_recv.at[n, j])

    def far_first(i, n):
        step = lax.div(i, 2)
        return n // 2 + jnp.where(lax.rem(i, 2) == 0, step, -step)

    def to_col(src_of, dst, n):
        def body(i, carry):
            peer = lax.rem(c + far_first(i, C), C)
            send(src_of(peer), dst, many_send.at[n], many_recv.at[n], col=peer)
            return carry

        lax.fori_loop(1, C, body, 0)

    def to_row(src_of, dst, n):
        def body(i, carry):
            peer = lax.rem(r + far_first(i, R), R)
            send(src_of(peer), dst, many_send.at[n], many_recv.at[n], row=peer)
            return carry

        lax.fori_loop(1, R, body, 0)

    def to_z(buf, n):
        def body(i, carry):
            send(buf.at[k, z], buf.at[k, z], many_send.at[n], many_recv.at[n], row=row_of(z + i, k))
            return carry

        lax.fori_loop(1, Z, body, 0)

    def z_to_sib(buf, n, m):
        got(buf.at[0, pl.ds(0, Z - 1)], many_recv.at[n])
        send(buf.at[k], buf.at[k], many_send.at[m], many_recv.at[m], row=row_of(z, 1 - k))

    lead = jnp.where(z == 0, 0, 1)
    for way in (lead, 1 - lead):

        @pl.when(jnp.where(way == 0, edges[1][1], edges[2][1]))
        def _(way=way):
            pl.semaphore_wait(near_sem.at[1 + way], 1)

        z_step(way, 1)
    edge(0)
    send(xbuf.at[k], xbuf.at[k], sib_send, sib_recv, row=row_of(z, 1 - k))
    greet(far_sem, (0, row_place), (0, col_place))

    p_index = c * PB + rows_p

    def onehot():
        return p_index.astype(F32) == wanted_ref[...]

    def student_scores():
        part = jnp.zeros((PB, 128), F32)
        order = [PR * (2 * zz + kk) + u for kk in range(2) for zz in range(Z) for u in range(PR)]
        rhs = jnp.concatenate([sqx[i] for i in order], axis=0).astype(BF)
        unit = lax.broadcasted_iota(jnp.int32, (PB, PB), 0) == lax.broadcasted_iota(jnp.int32, (PB, PB), 1)
        unit = unit.astype(BF)
        for g in range(3):
            wide = spt[:, :, 8 * PR * g : 8 * PR * (g + 1), :].reshape(2 * Z * 8 * PR, PB)
            back = nt(unit, wide).astype(BF)
            part = jnp.where(lane_group == g, nn(back, rhs), part)
        s = SCALE * spread(part)
        quarter = PB // GROUPS
        small = jnp.zeros((quarter, 128), F32)
        for g in range(GROUPS):
            small = jnp.where(lane_group == g, s[quarter * g : quarter * (g + 1)], small)
        top = jnp.max(s, axis=0, keepdims=True)
        mass = jnp.sum(jnp.exp(s - top), axis=0, keepdims=True)
        hit = jnp.sum(jnp.where(onehot(), s, 0.0), axis=0, keepdims=True)
        return s, small, jnp.where(lane_group == 0, top, jnp.where(lane_group == 1, mass, hit))

    def score_student():
        got(sqx.at[pl.ds(0, C - 1)], many_recv.at[0])
        got(spt.at[1 - k], many_recv.at[14])
        s, small, parts = student_scores()
        sbuf[...] = s
        zag[k, z] = small
        sst[c] = parts
        to_col(lambda peer: sst.at[c], sst.at[c], 3)
        to_z(zag, 6)
        to_row(lambda peer: sqx.at[pl.ds(PR * peer, PR)], sqr.at[r], 4)
        sqr[r] = sqx[pl.ds(PR * r, PR)]

    def only(v, g):
        return spread(jnp.where(lane_group == g, v, 0.0))

    def pack(dst, weights):
        hi, lo = split2(weights)
        table = spt[...].reshape(2 * Z * DR, PB)
        u = nn(jnp.concatenate([table, table], axis=1), jnp.concatenate([hi, lo], axis=0))
        for kk in range(2):
            for zz in range(Z):
                for uu in range(PR):
                    base = (kk * Z + zz) * DR + 8 * uu
                    piece = jnp.zeros((8, 128), F32)
                    for g in range(3):
                        at = base + 8 * PR * g
                        piece = jnp.where(lane_group == g, u[at : at + 8], piece)
                    dst[PR * (2 * zz + kk) + uu] = piece

    def softmax_parts(buf):
        rows = jnp.concatenate([buf[i] for i in range(C)], axis=0)
        tops = only(rows, 0)
        top = jnp.max(tops, axis=0, keepdims=True)
        weights = jnp.exp(tops - top)
        mass = only(jnp.sum(jnp.where(lane_group == 1, weights * rows, 0.0), axis=0, keepdims=True), 1)
        return top, mass, only(jnp.sum(rows, axis=0, keepdims=True), 2), weights

    def student_slopes():
        got(sst.at[pl.ds(0, C - 1)], many_recv.at[3])
        top, mass, hit, _ = softmax_parts(sst)
        zz_ = 2.0 * (jnp.exp(sbuf[...] - top) / mass) - jnp.where(onehot(), 1.0, 0.0)
        pack(upz, zz_)
        vbuf[c] = upz[c]
        to_col(lambda peer: upz.at[peer], vbuf.at[c], 5)
        sfin[r] = jnp.where(lane_group == 0, top, jnp.where(lane_group == 1, 1.0 / mass, wanted_ref[...]))
        to_row(lambda peer: sfin.at[r], sfin.at[r], 2)
        return top + jnp.log(mass), hit

    def owner(t, b):
        return 2 * (GROUPS * (t % (T // 2)) + b) + t // (T // 2)

    def row_vector(buf, t, g):
        tile = jnp.zeros((1, 128), F32)
        for b in range(GROUPS):
            v = buf[owner(t, b)]
            tile = jnp.where(lane_group == b, pltpu.roll(v, ((b - g) % GROUPS) * QB, 1) if b != g else v, tile)
        return tile

    def unpack_slopes():
        got(zag.at[1 - k], many_recv.at[7])
        got(sfin.at[pl.ds(0, R - 1)], many_recv.at[2])
        quarter = PB // GROUPS
        places = p_index.astype(F32)
        for t in range(T):
            for g in range(GROUPS):
                tile = jnp.zeros((quarter, 128), F32)
                for b in range(GROUPS):
                    rr = owner(t, b)
                    v = zag[rr % 2, rr // 2]
                    if b != g:
                        v = pltpu.roll(v, ((b - g) % GROUPS) * QB, 1)
                    tile = jnp.where(lane_group == b, v, tile)
                zfull[t, quarter * g : quarter * (g + 1)] = tile
            probs = jnp.exp(zfull[t] - row_vector(sfin, t, 0)) * row_vector(sfin, t, 1)
            zfull[t] = 2.0 * probs - jnp.where(places == row_vector(sfin, t, 2), 1.0, 0.0)

    def unpack_queries():
        got(sqr.at[pl.ds(0, R - 1)], many_recv.at[4])
        tiles = []
        for t in range(T):
            rows = []
            for u in range(PR):
                for g in range(3):
                    tile = jnp.zeros((8, 128), F32)
                    for b in range(GROUPS):
                        v = sqr[owner(t, b), u]
                        if b != g:
                            v = pltpu.roll(v, ((b - g) % GROUPS) * QB, 1)
                        tile = jnp.where(lane_group == b, v, tile)
                    rows.append(tile)
            tiles.append(jnp.concatenate(rows, axis=0).astype(BF))
        return tiles

    def turn(n, w):
        way, s = levels[n][w]
        z_got(way, s)
        if s < half - 1:
            z_step(way, s + 1)
        if n == half - 2:

            @pl.when(way == 0)
            def _():
                z_step(0, half)

        if n == 0 and w == 0:
            for e in (3, 4, 5, 6):
                edge(e)
        xy_step(numbers[n][w])

    turn(0, 0)
    turn(0, 1)
    got(xbuf.at[1 - k], sib_recv)
    tblk[z, 1 - k] = maxsim(xbuf[1 - k], z)
    town[z] = tblk[z]

    @pl.when(row_place + col_place < R + C - 2)
    def _():
        pl.semaphore_wait(far_sem, R - 1 - row_place + C - 1 - col_place)

    to_col(lambda peer: sqx.at[c], sqx.at[c], 0)
    to_z(spt, 1)
    last = len(blocks) - 1
    for j in range(len(blocks)):
        n, w = j // 2 + 1, j % 2
        if n < half - 1:
            turn(n, w)
        if j == min(3, last - 1):
            z_to_sib(spt, 1, 14)
        if j == min(4, last):
            turn(half - 1, 0)
            score_student()
        xy_got(j)
        teach(block(*blocks[j]))

    for t in range(T // 2):
        tile = tblk[GROUPS * t]
        for b in range(1, GROUPS):
            tile = jnp.where(lane_group == b, tblk[GROUPS * t + b], tile)
        tag[k, z, t] = tile
    student_lse, hit = student_slopes()
    z_to_sib(zag, 6, 7)
    got(tblk.at[pl.ds(0, Z - 1)], many_recv.at[12])
    t_own = town[...].reshape(PB, 128)
    top = jnp.max(t_own, axis=0, keepdims=True)
    e = jnp.exp(t_own - top)
    mass = jnp.sum(e, axis=0, keepdims=True)
    cross = jnp.sum(e * (t_own - sbuf[...]), axis=0, keepdims=True)
    tst[c] = jnp.where(lane_group == 0, top, jnp.where(lane_group == 1, mass, cross))
    to_col(lambda peer: tst.at[c], tst.at[c], 13)
    pack(upt, e)
    ubuf[c] = upt[c]

    @pl.when(k == 0)
    def _():
        to_col(lambda peer: upt.at[peer], ubuf.at[c], 10)

    to_z(tag, 8)
    sq_tiles = unpack_queries()
    got(vbuf.at[pl.ds(0, C - 1)], many_recv.at[5])
    v_sum = functools.reduce(jnp.add, [vbuf[i] for i in range(C)])
    unpack_slopes()

    got(tst.at[pl.ds(0, C - 1)], many_recv.at[13])
    top, mass, _, weights = softmax_parts(tst)
    rows = jnp.concatenate([tst[i] for i in range(C)], axis=0)
    cross = only(jnp.sum(weights * rows, axis=0, keepdims=True), 2)
    inverse = 1.0 / mass
    per_query = cross * inverse - (top + jnp.log(mass)) + 2.0 * student_lse - hit
    fin[r] = jnp.where(lane_group == 0, top, jnp.where(lane_group == 1, inverse, per_query))
    to_row(lambda peer: fin.at[r], fin.at[r], 11)

    @pl.when(k == 1)
    def _():
        to_col(lambda peer: upt.at[peer], ubuf.at[c], 10)

    z_to_sib(tag, 8, 9)
    got(ubuf.at[pl.ds(0, C - 1)], many_recv.at[10])
    acc = jnp.zeros((8, 128), F32)
    for i in range(C):
        acc = acc + weights[i : i + 1] * ubuf[i]
    grads = (SCALE / total) * (v_sum - acc * inverse)
    for g in range(3):
        qg_ref[8 * g : 8 * g + 8, :] = (pltpu.roll(grads, 128 - QB * g, 1) if g else grads)[:, 0:QB]
    got(tag.at[1 - k], many_recv.at[9])

    got(fin.at[pl.ds(0, R - 1)], many_recv.at[11])
    grads = jnp.zeros((DR, PB), F32)
    per_query = jnp.zeros((1, 128), F32)
    for t in range(T):
        tops = row_vector(fin, t, 0)
        inverses = row_vector(fin, t, 1)
        for b in range(GROUPS):
            per_query = per_query + jnp.where(lane_group == 2, fin[owner(t, b)], 0.0)
        slopes = zfull[t] - jnp.exp(tag[t // (T // 2), :, t % (T // 2)].reshape(PB, 128) - tops) * inverses
        hi, lo = split2(slopes)
        grads = grads + nt(jnp.concatenate([sq_tiles[t]] * 2, axis=1), jnp.concatenate([hi, lo], axis=1))
    pg_ref[...] = grads * (SCALE / total)
    loss_ref[...] = jnp.zeros((1, 1), F32) + jnp.sum(per_query) / total

    for s in range(1, half + 1):
        left(qbuf.at[z, mine], z_send.at[0, s - 1])
        if s < half:
            left(qbuf.at[z, mine], z_send.at[1, s - 1])
    for j in range(len(blocks)):
        for n, part in enumerate((mine, mine, mine_a, mine_b)):
            left(qbuf.at[z, part], xy_send.at[n, j])
    left(xbuf.at[k], sib_send)
    for n, buf, count in ((0, sqx, C), (2, sfin, R), (13, tst, C), (3, sst, C), (5, upz, C), (10, upt, C), (4, sqr, R), (11, fin, R), (12, tblk, Z)):
        left(buf.at[pl.ds(0, count - 1)], many_send.at[n])
    for n, m, buf in ((1, 14, spt), (6, 7, zag), (8, 9, tag)):
        left(buf.at[0, pl.ds(0, Z - 1)], many_send.at[n])
        left(buf.at[0], many_send.at[m])


def shards(query_tokens, query_lengths, passage_tokens, passage_lengths, student_queries, student_passages, positives):
    R = lax.axis_size("row")
    C = lax.axis_size("col")
    Z = R // 2
    L = query_tokens.shape[1]
    LP = passage_tokens.shape[1]
    PB = 8 * R
    PR = C // R
    DR = student_passages.shape[1]
    T = R // GROUPS
    hops = Z - 1
    dma = pltpu.SemaphoreType.DMA
    vmem = pl.BlockSpec(memory_space=pltpu.VMEM)
    hbm = pl.BlockSpec(memory_space=pltpu.HBM)
    pg, qg, loss = pl.pallas_call(
        functools.partial(kernel, R, C),
        out_shape=(
            jax.ShapeDtypeStruct((DR, PB), F32),
            jax.ShapeDtypeStruct((24, QB), F32),
            jax.ShapeDtypeStruct((1, 1), F32),
        ),
        in_specs=[hbm] * 7,
        out_specs=(vmem, vmem, vmem),
        scratch_shapes=[
            pltpu.SMEM((QB,), jnp.int32),
            pltpu.SMEM((8,), jnp.int32),
            pltpu.SMEM((QB,), jnp.int32),
            pltpu.VMEM((1, 128), F32),
            pltpu.VMEM((24, QB), BF),
            pltpu.VMEM((DR, PB), BF),
            pltpu.VMEM((QB, L, 128), BF),
            pltpu.VMEM((8, LP, 128), BF),
            pltpu.VMEM((Z, QB * L, 128), BF),
            pltpu.VMEM((2, LP * 8, 128), BF),
            pltpu.VMEM((C, 8, 128), F32),
            pltpu.VMEM((2, Z, DR, PB), BF),
            pltpu.VMEM((C, 1, 128), F32),
            pltpu.VMEM((PB, 128), F32),
            pltpu.VMEM((C, 8, 128), F32),
            pltpu.VMEM((C, 8, 128), F32),
            pltpu.VMEM((2, Z, PB // GROUPS, 128), F32),
            pltpu.VMEM((T, PB, 128), F32),
            pltpu.VMEM((R, PR, 8, 128), F32),
            pltpu.VMEM((Z, 2, 8, 128), F32),
            pltpu.VMEM((Z, 2, 8, 128), F32),
            pltpu.VMEM((2, Z, T // 2, 2, 8, 128), F32),
            pltpu.VMEM((C, 8, 128), F32),
            pltpu.VMEM((C, 8, 128), F32),
            pltpu.VMEM((C, 1, 128), F32),
            pltpu.VMEM((R, 1, 128), F32),
            pltpu.VMEM((R, 1, 128), F32),
            dma((7,)),
            pltpu.SemaphoreType.REGULAR((7,)),
            pltpu.SemaphoreType.REGULAR,
            dma((2, Z // 2)),
            dma((2, Z // 2)),
            dma((4, hops)),
            dma((4, hops)),
            dma,
            dma,
            dma((15,)),
            dma((15,)),
        ],
        compiler_params=pltpu.CompilerParams(
            collective_id=0, has_side_effects=True, vmem_limit_bytes=64 * 1024 * 1024
        ),
        name="distill",
    )(query_tokens, query_lengths, passage_tokens, passage_lengths, student_queries.T, student_passages.T, positives)
    return qg.T, pg.T, loss.reshape(())


def solution(mesh):
    return jax.shard_map(
        shards,
        mesh=mesh,
        in_specs=(
            P("row", None, None),
            P("row"),
            P(("col", "row"), None, None),
            P(("col", "row")),
            P("row", "col"),
            P("col", "row"),
            P("row"),
        ),
        out_specs=(P("row", "col"), P("col", "row"), P()),
        check_vma=False,
    )
```

```python
import functools

import jax
import jax.numpy as jnp
from jax import lax
from jax.experimental import pallas as pl
from jax.experimental.pallas import tpu as pltpu
from jax.sharding import PartitionSpec as P

MESH = pl.DeviceIdType.MESH
SCALE = 4.0
X_CHIPS = 4
QB = 32
GROUPS = 128 // QB
BF = jnp.bfloat16
F32 = jnp.float32


def nt(a, b):
    return lax.dot_general(a, b, (((1,), (1,)), ((), ())), preferred_element_type=F32)


def nn(a, b):
    return lax.dot_general(a, b, (((1,), (0,)), ((), ())), preferred_element_type=F32)


def split2(v):
    hi = v.astype(BF)
    return hi, (v - hi.astype(F32)).astype(BF)


def spread(v):
    v = v + pltpu.roll(v, 64, 1)
    return v + pltpu.roll(v, 32, 1)


def kernel(
    R,
    C,
    qt_hbm,
    qlen_hbm,
    pt_hbm,
    plen_hbm,
    sq_hbm,
    sp_hbm,
    pos_hbm,
    pg_ref,
    qg_ref,
    loss_ref,
    qlen_ref,
    plen_ref,
    pos_ref,
    wanted_ref,
    sq_ref,
    sp_ref,
    qraw,
    praw,
    qbuf,
    xbuf,
    sqx,
    spt,
    sst,
    sbuf,
    upz,
    vbuf,
    zag,
    zfull,
    sqr,
    tblk,
    town,
    tag,
    upt,
    ubuf,
    tst,
    sfin,
    fin,
    in_sem,
    near_sem,
    far_sem,
    z_send,
    z_recv,
    xy_send,
    xy_recv,
    sib_send,
    sib_recv,
    many_send,
    many_recv,
):
    Z = R // 2
    XC = min(X_CHIPS, C)
    YC = C // XC
    L = qt_hbm.shape[1]
    LP = pt_hbm.shape[1]
    N = QB * L
    SL = N // 4
    HALF = SL // 2
    PB = 8 * R
    PR = C // R
    DR = 24 * PR
    T = R // GROUPS
    total = QB * R

    r = lax.axis_index("row")
    c = lax.axis_index("col")
    z = lax.div(r, 2)
    k = lax.rem(r, 2)
    x = lax.rem(c, XC)
    y = lax.div(c, XC)
    color = lax.rem(jnp.where(k == 0, x + 2 * y, 2 * x + y), 4)

    def row_of(zz, kk):
        return lax.rem(zz + 2 * Z, Z) * 2 + kk

    def col_of(xx, yy):
        return lax.rem(yy + YC, YC) * XC + lax.rem(xx + XC, XC)

    def send(src, dst, s_sem, r_sem, **where):
        pltpu.make_async_remote_copy(
            src_ref=src, dst_ref=dst, send_sem=s_sem, recv_sem=r_sem, device_id=where, device_id_type=MESH
        ).start()

    def got(dst, r_sem):
        pltpu.make_async_remote_copy(
            src_ref=dst, dst_ref=dst, send_sem=r_sem, recv_sem=r_sem, device_id={"row": r}, device_id_type=MESH
        ).wait_recv()

    def left(src, s_sem):
        pltpu.make_async_remote_copy(
            src_ref=src, dst_ref=src, send_sem=s_sem, recv_sem=s_sem, device_id={"row": r}, device_id_type=MESH
        ).wait_send()

    barrier = pltpu.get_barrier_semaphore()

    def row_rank(rr):
        return lax.div(rr, 2) * 2 + 1 - lax.rem(rr, 2)

    def col_rank(cc):
        yy = lax.div(cc, XC)
        return jnp.where(yy < YC // 2, yy, YC // 2 + YC - 1 - yy) * XC + lax.rem(cc, XC)

    row_place, col_place = row_rank(r), col_rank(c)
    edges = (
        ({"row": row_of(z, 1 - k)}, row_rank(row_of(z, 1 - k)) > row_place, 0),
        ({"row": row_of(z + 1, k)}, row_rank(row_of(z + 1, k)) > row_place, 2),
        ({"row": row_of(z - 1, k)}, row_rank(row_of(z - 1, k)) > row_place, 1),
        ({"col": col_of(x + 1, y)}, col_rank(col_of(x + 1, y)) > col_place, 4),
        ({"col": col_of(x - 1, y)}, col_rank(col_of(x - 1, y)) > col_place, 3),
        ({"col": col_of(x, y + 1)}, col_rank(col_of(x, y + 1)) > col_place, 6),
        ({"col": col_of(x, y - 1)}, col_rank(col_of(x, y - 1)) > col_place, 5),
    )

    def row_at(place):
        return lax.div(place, 2) * 2 + 1 - lax.rem(place, 2)

    def col_at(place):
        yy = lax.div(place, XC)
        return jnp.where(yy < YC // 2, yy, YC // 2 + YC - 1 - yy) * XC + lax.rem(place, XC)

    def greet(sem, row_places, col_places):
        def rows(i, carry):
            pl.semaphore_signal(sem, inc=1, device_id={"row": row_at(i)}, device_id_type=MESH)
            return carry

        def cols(i, carry):
            pl.semaphore_signal(sem, inc=1, device_id={"col": col_at(i)}, device_id_type=MESH)
            return carry

        lax.fori_loop(*row_places, rows, 0)
        lax.fori_loop(*col_places, cols, 0)

    def edge(n):
        @pl.when(edges[n][1])
        def _():
            pl.semaphore_wait(near_sem.at[n], 1)

    inputs = [
        pltpu.make_async_copy(src, dst, in_sem.at[n])
        for n, (src, dst) in enumerate(
            (
                (qt_hbm, qraw),
                (qlen_hbm, qlen_ref),
                (pt_hbm, praw),
                (plen_hbm, plen_ref),
                (sq_hbm, sq_ref),
                (sp_hbm, sp_ref),
                (pos_hbm, pos_ref),
            )
        )
    ]
    for copy in inputs:
        copy.start()
    greet(barrier, (row_place + 1, R), (col_place + 1, C))

    rows_p = lax.broadcasted_iota(jnp.int32, (PB, 128), 0)
    lane = lax.broadcasted_iota(jnp.int32, (1, 128), 1)
    lane_group = lax.div(lane, QB)

    inputs[0].wait()
    inputs[1].wait()
    slot = lax.broadcasted_iota(jnp.int32, (L, 128), 0)
    q32 = jnp.stack(
        [jnp.where(slot < qlen_ref[i], qraw[i].astype(F32), 0.0) for i in range(QB)], axis=0
    )
    qbuf[z] = jnp.swapaxes(q32, 0, 1).reshape(N, 128).astype(BF)


    inputs[4].wait()
    inputs[5].wait()
    qa = lax.broadcasted_iota(jnp.int32, (QB, 128), 0)
    qb = lax.broadcasted_iota(jnp.int32, (QB, 128), 1)
    sq_wide = nn(sq_ref[...], (qa == lax.rem(qb, QB)).astype(BF))
    packed = jnp.zeros((8, 128), F32)
    for g in range(3):
        packed = jnp.where(lane_group == g, sq_wide[8 * g : 8 * g + 8], packed)
    sqx[c] = packed
    sp_wide = sp_ref[...].astype(F32)
    spt[k, z] = jnp.concatenate(
        [sp_wide[24 * u + 8 * g : 24 * u + 8 * g + 8] for g in range(3) for u in range(PR)], axis=0
    ).astype(BF)

    inputs[6].wait()
    wanted = jnp.zeros((1, 128), F32)
    within = lax.rem(lane, QB)
    for i in range(QB):
        wanted = jnp.where(within == i, pos_ref[i].astype(F32), wanted)
    wanted_ref[...] = wanted

    inputs[2].wait()
    inputs[3].wait()
    pslot = lax.broadcasted_iota(jnp.int32, (LP, 128), 0)
    p32 = []
    for i in range(8):
        rows = praw[i].astype(F32)
        p32.append(jnp.where(pslot < plen_ref[i], rows, rows[0:1]))
    xbuf[k] = jnp.swapaxes(jnp.stack(p32, axis=0), 0, 1).reshape(LP * 8, 128).astype(BF)

    def maxsim(tokens, zz):
        s = nt(tokens, qbuf[zz])
        m = jnp.max(s.reshape(-1, LP, 8, N), axis=1).reshape(-1, N)
        acc = m[:, 0:128]
        for t in range(1, N // 128):
            acc = acc + m[:, 128 * t : 128 * t + 128]
        return spread(acc)

    def teach(zz):
        tblk[zz] = maxsim(xbuf[...].reshape(2 * LP * 8, 128), zz).reshape(2, 8, 128)
        send(tblk.at[zz], town.at[z], many_send.at[12], many_recv.at[12], row=row_of(zz, k))

    tblk[z, k] = maxsim(xbuf[k], z)

    @pl.when(row_place + col_place > 0)
    def _():
        pl.semaphore_wait(barrier, row_place + col_place)

    for peer, later, back in edges:

        @pl.when(jnp.logical_not(later))
        def _(peer=peer, back=back):
            pl.semaphore_signal(near_sem.at[back], inc=1, device_id=peer, device_id_type=MESH)


    mine = pl.ds(pl.multiple_of(color * SL, SL), SL)
    mine_a = pl.ds(pl.multiple_of(color * SL, HALF), HALF)
    mine_b = pl.ds(pl.multiple_of(color * SL + HALF, HALF), HALF)

    half = Z // 2
    ways = (jnp.where(z < 2, 1, 0), jnp.where(z < 2, 0, 1))
    levels = [[(w, s) for w in ways] for s in range(1, half)] + [[(0, half)]]
    numbers = [[2 * n + w for w in range(len(level))] for n, level in enumerate(levels)]

    def block(way, s):
        return lax.rem(z + (2 * way - 1) * s + Z, Z)

    blocks = [(way, s) for level in levels for way, s in level]

    def z_step(way, s):
        b = block(way, s - 1)
        send(
            qbuf.at[b, mine], qbuf.at[b, mine], z_send.at[way, s - 1], z_recv.at[way, s - 1], row=row_of(z + 1 - 2 * way, k)
        )

    def z_got(way, s):
        got(qbuf.at[block(way, s), mine], z_recv.at[way, s - 1])

    def xy_regions():
        one = lax.rem(color + 3, 4) * SL
        two = lax.rem(color + 1, 4) * SL
        far = lax.rem(color + 2, 4) * SL
        return (
            pl.ds(pl.multiple_of(one, SL), SL),
            pl.ds(pl.multiple_of(two, SL), SL),
            pl.ds(pl.multiple_of(far, HALF), HALF),
            pl.ds(pl.multiple_of(far + HALF, HALF), HALF),
        )

    def xy_step(j):
        b = block(*blocks[j])
        beside = (col_of(x + 1, y), col_of(x - 1, y))
        above = (col_of(x, y + 1), col_of(x, y - 1))
        to = [jnp.where(k == 0, a, b) for a, b in zip(beside + above, above + beside)]
        for n, (part, peer) in enumerate(zip((mine, mine, mine_a, mine_b), to)):
            send(qbuf.at[b, part], qbuf.at[b, part], xy_send.at[n, j], xy_recv.at[n, j], col=peer)

    def xy_got(j):
        b = block(*blocks[j])
        for n, part in enumerate(xy_regions()):
            got(qbuf.at[b, part], xy_recv.at[n, j])

    def far_first(i, n):
        step = lax.div(i, 2)
        return n // 2 + jnp.where(lax.rem(i, 2) == 0, step, -step)

    def to_col(src_of, dst, n):
        def body(i, carry):
            peer = lax.rem(c + far_first(i, C), C)
            send(src_of(peer), dst, many_send.at[n], many_recv.at[n], col=peer)
            return carry

        lax.fori_loop(1, C, body, 0)

    def to_row(src_of, dst, n):
        def body(i, carry):
            peer = lax.rem(r + far_first(i, R), R)
            send(src_of(peer), dst, many_send.at[n], many_recv.at[n], row=peer)
            return carry

        lax.fori_loop(1, R, body, 0)

    def to_z(buf, n):
        def body(i, carry):
            send(buf.at[k, z], buf.at[k, z], many_send.at[n], many_recv.at[n], row=row_of(z + i, k))
            return carry

        lax.fori_loop(1, Z, body, 0)

    def z_to_sib(buf, n, m):
        got(buf.at[0, pl.ds(0, Z - 1)], many_recv.at[n])
        send(buf.at[k], buf.at[k], many_send.at[m], many_recv.at[m], row=row_of(z, 1 - k))

    lead = jnp.where(z == 0, 0, 1)
    for way in (lead, 1 - lead):

        @pl.when(jnp.where(way == 0, edges[1][1], edges[2][1]))
        def _(way=way):
            pl.semaphore_wait(near_sem.at[1 + way], 1)

        z_step(way, 1)
    edge(0)
    send(xbuf.at[k], xbuf.at[k], sib_send, sib_recv, row=row_of(z, 1 - k))
    greet(far_sem, (0, row_place), (0, col_place))

    p_index = c * PB + rows_p

    def onehot():
        return p_index.astype(F32) == wanted_ref[...]

    def student_scores():
        part = jnp.zeros((PB, 128), F32)
        order = [PR * (2 * zz + kk) + u for kk in range(2) for zz in range(Z) for u in range(PR)]
        rhs = jnp.concatenate([sqx[i] for i in order], axis=0).astype(BF)
        unit = lax.broadcasted_iota(jnp.int32, (PB, PB), 0) == lax.broadcasted_iota(jnp.int32, (PB, PB), 1)
        unit = unit.astype(BF)
        for g in range(3):
            wide = spt[:, :, 8 * PR * g : 8 * PR * (g + 1), :].reshape(2 * Z * 8 * PR, PB)
            back = nt(unit, wide).astype(BF)
            part = jnp.where(lane_group == g, nn(back, rhs), part)
        s = SCALE * spread(part)
        quarter = PB // GROUPS
        small = jnp.zeros((quarter, 128), F32)
        for g in range(GROUPS):
            small = jnp.where(lane_group == g, s[quarter * g : quarter * (g + 1)], small)
        top = jnp.max(s, axis=0, keepdims=True)
        mass = jnp.sum(jnp.exp(s - top), axis=0, keepdims=True)
        hit = jnp.sum(jnp.where(onehot(), s, 0.0), axis=0, keepdims=True)
        return s, small, jnp.where(lane_group == 0, top, jnp.where(lane_group == 1, mass, hit))

    def score_student():
        got(sqx.at[pl.ds(0, C - 1)], many_recv.at[0])
        got(spt.at[1 - k], many_recv.at[14])
        s, small, parts = student_scores()
        sbuf[...] = s
        zag[k, z] = small
        sst[c] = parts
        to_col(lambda peer: sst.at[c], sst.at[c], 3)
        to_z(zag, 6)
        to_row(lambda peer: sqx.at[pl.ds(PR * peer, PR)], sqr.at[r], 4)
        sqr[r] = sqx[pl.ds(PR * r, PR)]

    def only(v, g):
        return spread(jnp.where(lane_group == g, v, 0.0))

    def pack(dst, weights):
        hi, lo = split2(weights)
        table = spt[...].reshape(2 * Z * DR, PB)
        u = nn(jnp.concatenate([table, table], axis=1), jnp.concatenate([hi, lo], axis=0))
        for kk in range(2):
            for zz in range(Z):
                for uu in range(PR):
                    base = (kk * Z + zz) * DR + 8 * uu
                    piece = jnp.zeros((8, 128), F32)
                    for g in range(3):
                        at = base + 8 * PR * g
                        piece = jnp.where(lane_group == g, u[at : at + 8], piece)
                    dst[PR * (2 * zz + kk) + uu] = piece

    def softmax_parts(buf):
        rows = jnp.concatenate([buf[i] for i in range(C)], axis=0)
        tops = only(rows, 0)
        top = jnp.max(tops, axis=0, keepdims=True)
        weights = jnp.exp(tops - top)
        mass = only(jnp.sum(jnp.where(lane_group == 1, weights * rows, 0.0), axis=0, keepdims=True), 1)
        return top, mass, only(jnp.sum(rows, axis=0, keepdims=True), 2), weights

    def student_slopes():
        got(sst.at[pl.ds(0, C - 1)], many_recv.at[3])
        top, mass, hit, _ = softmax_parts(sst)
        zz_ = 2.0 * (jnp.exp(sbuf[...] - top) / mass) - jnp.where(onehot(), 1.0, 0.0)
        pack(upz, zz_)
        vbuf[c] = upz[c]
        to_col(lambda peer: upz.at[peer], vbuf.at[c], 5)
        sfin[r] = jnp.where(lane_group == 0, top, jnp.where(lane_group == 1, 1.0 / mass, wanted_ref[...]))
        to_row(lambda peer: sfin.at[r], sfin.at[r], 2)
        return top + jnp.log(mass), hit

    def owner(t, b):
        return 2 * (GROUPS * (t % (T // 2)) + b) + t // (T // 2)

    def row_vector(buf, t, g):
        tile = jnp.zeros((1, 128), F32)
        for b in range(GROUPS):
            v = buf[owner(t, b)]
            tile = jnp.where(lane_group == b, pltpu.roll(v, ((b - g) % GROUPS) * QB, 1) if b != g else v, tile)
        return tile

    def unpack_slopes():
        got(zag.at[1 - k], many_recv.at[7])
        got(sfin.at[pl.ds(0, R - 1)], many_recv.at[2])
        quarter = PB // GROUPS
        places = p_index.astype(F32)
        for t in range(T):
            for g in range(GROUPS):
                tile = jnp.zeros((quarter, 128), F32)
                for b in range(GROUPS):
                    rr = owner(t, b)
                    v = zag[rr % 2, rr // 2]
                    if b != g:
                        v = pltpu.roll(v, ((b - g) % GROUPS) * QB, 1)
                    tile = jnp.where(lane_group == b, v, tile)
                zfull[t, quarter * g : quarter * (g + 1)] = tile
            probs = jnp.exp(zfull[t] - row_vector(sfin, t, 0)) * row_vector(sfin, t, 1)
            zfull[t] = 2.0 * probs - jnp.where(places == row_vector(sfin, t, 2), 1.0, 0.0)

    def unpack_queries():
        got(sqr.at[pl.ds(0, R - 1)], many_recv.at[4])
        tiles = []
        for t in range(T):
            rows = []
            for u in range(PR):
                for g in range(3):
                    tile = jnp.zeros((8, 128), F32)
                    for b in range(GROUPS):
                        v = sqr[owner(t, b), u]
                        if b != g:
                            v = pltpu.roll(v, ((b - g) % GROUPS) * QB, 1)
                        tile = jnp.where(lane_group == b, v, tile)
                    rows.append(tile)
            tiles.append(jnp.concatenate(rows, axis=0).astype(BF))
        return tiles

    def turn(n, w):
        way, s = levels[n][w]
        z_got(way, s)
        if s < half - 1:
            z_step(way, s + 1)
        if n == half - 2:

            @pl.when(way == 0)
            def _():
                z_step(0, half)

        if n == 0 and w == 0:
            for e in (3, 4, 5, 6):
                edge(e)
        xy_step(numbers[n][w])

    turn(0, 0)
    turn(0, 1)
    got(xbuf.at[1 - k], sib_recv)
    tblk[z, 1 - k] = maxsim(xbuf[1 - k], z)
    town[z] = tblk[z]

    @pl.when(row_place + col_place < R + C - 2)
    def _():
        pl.semaphore_wait(far_sem, R - 1 - row_place + C - 1 - col_place)

    to_z(spt, 1)
    steps = [0, *range(2, len(blocks)), 1]
    for i, j in enumerate(steps):
        if i == 0:
            if half > 2:
                turn(1, 0)
            to_col(lambda peer: sqx.at[c], sqx.at[c], 0)
            if half > 2:
                turn(1, 1)
        if i in (1, 2) and half > 3:
            turn(2, i - 1)
        if i == max(1, len(steps) - 4):
            z_to_sib(spt, 1, 14)
        if i == max(1, len(steps) - 3):
            turn(half - 1, 0)
            score_student()
        xy_got(j)
        teach(block(*blocks[j]))

    for t in range(T // 2):
        tile = tblk[GROUPS * t]
        for b in range(1, GROUPS):
            tile = jnp.where(lane_group == b, tblk[GROUPS * t + b], tile)
        tag[k, z, t] = tile
    student_lse, hit = student_slopes()
    z_to_sib(zag, 6, 7)
    got(tblk.at[pl.ds(0, Z - 1)], many_recv.at[12])
    t_own = town[...].reshape(PB, 128)
    top = jnp.max(t_own, axis=0, keepdims=True)
    e = jnp.exp(t_own - top)
    mass = jnp.sum(e, axis=0, keepdims=True)
    cross = jnp.sum(e * (t_own - sbuf[...]), axis=0, keepdims=True)
    tst[c] = jnp.where(lane_group == 0, top, jnp.where(lane_group == 1, mass, cross))
    to_col(lambda peer: tst.at[c], tst.at[c], 13)
    pack(upt, e)
    ubuf[c] = upt[c]

    @pl.when(k == 0)
    def _():
        to_col(lambda peer: upt.at[peer], ubuf.at[c], 10)

    to_z(tag, 8)
    sq_tiles = unpack_queries()
    got(vbuf.at[pl.ds(0, C - 1)], many_recv.at[5])
    v_sum = functools.reduce(jnp.add, [vbuf[i] for i in range(C)])
    unpack_slopes()

    got(tst.at[pl.ds(0, C - 1)], many_recv.at[13])
    top, mass, _, weights = softmax_parts(tst)
    rows = jnp.concatenate([tst[i] for i in range(C)], axis=0)
    cross = only(jnp.sum(weights * rows, axis=0, keepdims=True), 2)
    inverse = 1.0 / mass
    per_query = cross * inverse - (top + jnp.log(mass)) + 2.0 * student_lse - hit
    fin[r] = jnp.where(lane_group == 0, top, jnp.where(lane_group == 1, inverse, per_query))
    to_row(lambda peer: fin.at[r], fin.at[r], 11)

    @pl.when(k == 1)
    def _():
        to_col(lambda peer: upt.at[peer], ubuf.at[c], 10)

    z_to_sib(tag, 8, 9)
    got(ubuf.at[pl.ds(0, C - 1)], many_recv.at[10])
    acc = jnp.zeros((8, 128), F32)
    for i in range(C):
        acc = acc + weights[i : i + 1] * ubuf[i]
    grads = (SCALE / total) * (v_sum - acc * inverse)
    for g in range(3):
        qg_ref[8 * g : 8 * g + 8, :] = (pltpu.roll(grads, 128 - QB * g, 1) if g else grads)[:, 0:QB]
    got(tag.at[1 - k], many_recv.at[9])

    got(fin.at[pl.ds(0, R - 1)], many_recv.at[11])
    grads = jnp.zeros((DR, PB), F32)
    per_query = jnp.zeros((1, 128), F32)
    for t in range(T):
        tops = row_vector(fin, t, 0)
        inverses = row_vector(fin, t, 1)
        for b in range(GROUPS):
            per_query = per_query + jnp.where(lane_group == 2, fin[owner(t, b)], 0.0)
        slopes = zfull[t] - jnp.exp(tag[t // (T // 2), :, t % (T // 2)].reshape(PB, 128) - tops) * inverses
        hi, lo = split2(slopes)
        grads = grads + nt(jnp.concatenate([sq_tiles[t]] * 2, axis=1), jnp.concatenate([hi, lo], axis=1))
    pg_ref[...] = grads * (SCALE / total)
    loss_ref[...] = jnp.zeros((1, 1), F32) + jnp.sum(per_query) / total

    for s in range(1, half + 1):
        left(qbuf.at[z, mine], z_send.at[0, s - 1])
        if s < half:
            left(qbuf.at[z, mine], z_send.at[1, s - 1])
    for j in range(len(blocks)):
        for n, part in enumerate((mine, mine, mine_a, mine_b)):
            left(qbuf.at[z, part], xy_send.at[n, j])
    left(xbuf.at[k], sib_send)
    for n, buf, count in ((0, sqx, C), (2, sfin, R), (13, tst, C), (3, sst, C), (5, upz, C), (10, upt, C), (4, sqr, R), (11, fin, R), (12, tblk, Z)):
        left(buf.at[pl.ds(0, count - 1)], many_send.at[n])
    for n, m, buf in ((1, 14, spt), (6, 7, zag), (8, 9, tag)):
        left(buf.at[0, pl.ds(0, Z - 1)], many_send.at[n])
        left(buf.at[0], many_send.at[m])


def hand_over(pg_ref, qg_ref, loss_ref, pg_out, qg_out, loss_out):
    pg_out[...] = pg_ref[...]
    qg_out[...] = qg_ref[...]
    loss_out[...] = loss_ref[...]


def shards(query_tokens, query_lengths, passage_tokens, passage_lengths, student_queries, student_passages, positives):
    R = lax.axis_size("row")
    C = lax.axis_size("col")
    Z = R // 2
    L = query_tokens.shape[1]
    LP = passage_tokens.shape[1]
    PB = 8 * R
    PR = C // R
    DR = student_passages.shape[1]
    T = R // GROUPS
    hops = Z - 1
    dma = pltpu.SemaphoreType.DMA
    vmem = pl.BlockSpec(memory_space=pltpu.VMEM)
    hbm = pl.BlockSpec(memory_space=pltpu.HBM)
    pg, qg, loss = pl.pallas_call(
        functools.partial(kernel, R, C),
        out_shape=(
            jax.ShapeDtypeStruct((DR, PB), F32),
            jax.ShapeDtypeStruct((24, QB), F32),
            jax.ShapeDtypeStruct((1, 1), F32),
        ),
        in_specs=[hbm] * 7,
        out_specs=(vmem, vmem, vmem),
        scratch_shapes=[
            pltpu.SMEM((QB,), jnp.int32),
            pltpu.SMEM((8,), jnp.int32),
            pltpu.SMEM((QB,), jnp.int32),
            pltpu.VMEM((1, 128), F32),
            pltpu.VMEM((24, QB), BF),
            pltpu.VMEM((DR, PB), BF),
            pltpu.VMEM((QB, L, 128), BF),
            pltpu.VMEM((8, LP, 128), BF),
            pltpu.VMEM((Z, QB * L, 128), BF),
            pltpu.VMEM((2, LP * 8, 128), BF),
            pltpu.VMEM((C, 8, 128), F32),
            pltpu.VMEM((2, Z, DR, PB), BF),
            pltpu.VMEM((C, 1, 128), F32),
            pltpu.VMEM((PB, 128), F32),
            pltpu.VMEM((C, 8, 128), F32),
            pltpu.VMEM((C, 8, 128), F32),
            pltpu.VMEM((2, Z, PB // GROUPS, 128), F32),
            pltpu.VMEM((T, PB, 128), F32),
            pltpu.VMEM((R, PR, 8, 128), F32),
            pltpu.VMEM((Z, 2, 8, 128), F32),
            pltpu.VMEM((Z, 2, 8, 128), F32),
            pltpu.VMEM((2, Z, T // 2, 2, 8, 128), F32),
            pltpu.VMEM((C, 8, 128), F32),
            pltpu.VMEM((C, 8, 128), F32),
            pltpu.VMEM((C, 1, 128), F32),
            pltpu.VMEM((R, 1, 128), F32),
            pltpu.VMEM((R, 1, 128), F32),
            dma((7,)),
            pltpu.SemaphoreType.REGULAR((7,)),
            pltpu.SemaphoreType.REGULAR,
            dma((2, Z // 2)),
            dma((2, Z // 2)),
            dma((4, hops)),
            dma((4, hops)),
            dma,
            dma,
            dma((15,)),
            dma((15,)),
        ],
        compiler_params=pltpu.CompilerParams(
            collective_id=0, has_side_effects=True, vmem_limit_bytes=64 * 1024 * 1024
        ),
        name="distill",
    )(query_tokens, query_lengths, passage_tokens, passage_lengths, student_queries.T, student_passages.T, positives)
    pg, qg, loss = pl.pallas_call(
        hand_over,
        out_shape=tuple(jax.ShapeDtypeStruct(a.shape, a.dtype) for a in (pg, qg, loss)),
        in_specs=[vmem] * 3,
        out_specs=(vmem, vmem, vmem),
        name="hand_over",
    )(pg, qg, loss)
    return qg.T, pg.T, loss.reshape(())


def solution(mesh):
    return jax.shard_map(
        shards,
        mesh=mesh,
        in_specs=(
            P("row", None, None),
            P("row"),
            P(("col", "row"), None, None),
            P(("col", "row")),
            P("row", "col"),
            P("col", "row"),
            P("row"),
        ),
        out_specs=(P("row", "col"), P("col", "row"), P()),
        check_vma=False,
    )
```

```python
import functools

import jax
import jax.numpy as jnp
from jax import lax
from jax.experimental import pallas as pl
from jax.experimental.pallas import tpu as pltpu
from jax.sharding import PartitionSpec as P

MESH = pl.DeviceIdType.MESH
SCALE = 4.0
X_CHIPS = 4
QB = 32
GROUPS = 128 // QB
BF = jnp.bfloat16
F32 = jnp.float32


def nt(a, b):
    return lax.dot_general(a, b, (((1,), (1,)), ((), ())), preferred_element_type=F32)


def nn(a, b):
    return lax.dot_general(a, b, (((1,), (0,)), ((), ())), preferred_element_type=F32)


def split2(v):
    hi = v.astype(BF)
    return hi, (v - hi.astype(F32)).astype(BF)


def spread(v):
    v = v + pltpu.roll(v, 64, 1)
    return v + pltpu.roll(v, 32, 1)


def kernel(
    R,
    C,
    qt_hbm,
    qlen_hbm,
    pt_hbm,
    plen_hbm,
    sq_ref,
    sp_hbm,
    pos_hbm,
    pg_ref,
    qg_ref,
    loss_ref,
    qlen_ref,
    plen_ref,
    pos_ref,
    wanted_ref,
    sp_ref,
    qraw,
    praw,
    qbuf,
    xbuf,
    sqx,
    spt,
    sst,
    sbuf,
    upz,
    vbuf,
    zag,
    zfull,
    sqr,
    tblk,
    town,
    tag,
    upt,
    ubuf,
    tst,
    sfin,
    fin,
    in_sem,
    near_sem,
    far_sem,
    z_send,
    z_recv,
    xy_send,
    xy_recv,
    sib_send,
    sib_recv,
    many_send,
    many_recv,
):
    Z = R // 2
    XC = min(X_CHIPS, C)
    YC = C // XC
    L = qt_hbm.shape[1]
    LP = pt_hbm.shape[1]
    N = QB * L
    SL = N // 4
    HALF = SL // 2
    PB = 8 * R
    PR = C // R
    DR = 24 * PR
    T = R // GROUPS
    total = QB * R

    r = lax.axis_index("row")
    c = lax.axis_index("col")
    z = lax.div(r, 2)
    k = lax.rem(r, 2)
    x = lax.rem(c, XC)
    y = lax.div(c, XC)
    color = lax.rem(jnp.where(k == 0, x + 2 * y, 2 * x + y), 4)

    def row_of(zz, kk):
        return lax.rem(zz + 2 * Z, Z) * 2 + kk

    def col_of(xx, yy):
        return lax.rem(yy + YC, YC) * XC + lax.rem(xx + XC, XC)

    def send(src, dst, s_sem, r_sem, **where):
        pltpu.make_async_remote_copy(
            src_ref=src, dst_ref=dst, send_sem=s_sem, recv_sem=r_sem, device_id=where, device_id_type=MESH
        ).start()

    def got(dst, r_sem):
        pltpu.make_async_remote_copy(
            src_ref=dst, dst_ref=dst, send_sem=r_sem, recv_sem=r_sem, device_id={"row": r}, device_id_type=MESH
        ).wait_recv()

    def left(src, s_sem):
        pltpu.make_async_remote_copy(
            src_ref=src, dst_ref=src, send_sem=s_sem, recv_sem=s_sem, device_id={"row": r}, device_id_type=MESH
        ).wait_send()

    barrier = pltpu.get_barrier_semaphore()

    def row_rank(rr):
        return lax.div(rr, 2) * 2 + 1 - lax.rem(rr, 2)

    def col_rank(cc):
        yy = lax.div(cc, XC)
        return jnp.where(yy < YC // 2, yy, YC // 2 + YC - 1 - yy) * XC + lax.rem(cc, XC)

    row_place, col_place = row_rank(r), col_rank(c)
    edges = (
        ({"row": row_of(z, 1 - k)}, row_rank(row_of(z, 1 - k)) > row_place, 0),
        ({"row": row_of(z + 1, k)}, row_rank(row_of(z + 1, k)) > row_place, 2),
        ({"row": row_of(z - 1, k)}, row_rank(row_of(z - 1, k)) > row_place, 1),
        ({"col": col_of(x + 1, y)}, col_rank(col_of(x + 1, y)) > col_place, 4),
        ({"col": col_of(x - 1, y)}, col_rank(col_of(x - 1, y)) > col_place, 3),
        ({"col": col_of(x, y + 1)}, col_rank(col_of(x, y + 1)) > col_place, 6),
        ({"col": col_of(x, y - 1)}, col_rank(col_of(x, y - 1)) > col_place, 5),
    )

    def row_at(place):
        return lax.div(place, 2) * 2 + 1 - lax.rem(place, 2)

    def col_at(place):
        yy = lax.div(place, XC)
        return jnp.where(yy < YC // 2, yy, YC // 2 + YC - 1 - yy) * XC + lax.rem(place, XC)

    def greet(sem, row_places, col_places):
        def rows(i, carry):
            pl.semaphore_signal(sem, inc=1, device_id={"row": row_at(i)}, device_id_type=MESH)
            return carry

        def cols(i, carry):
            pl.semaphore_signal(sem, inc=1, device_id={"col": col_at(i)}, device_id_type=MESH)
            return carry

        lax.fori_loop(*row_places, rows, 0)
        lax.fori_loop(*col_places, cols, 0)

    def edge(n):
        @pl.when(edges[n][1])
        def _():
            pl.semaphore_wait(near_sem.at[n], 1)

    inputs = [
        pltpu.make_async_copy(src, dst, in_sem.at[n])
        for n, (src, dst) in enumerate(
            (
                (qt_hbm, qraw),
                (qlen_hbm, qlen_ref),
                (pt_hbm, praw),
                (plen_hbm, plen_ref),
                (sp_hbm, sp_ref),
                (pos_hbm, pos_ref),
            )
        )
    ]
    for copy in inputs:
        copy.start()
    greet(barrier, (row_place + 1, R), (col_place + 1, C))

    rows_p = lax.broadcasted_iota(jnp.int32, (PB, 128), 0)
    lane = lax.broadcasted_iota(jnp.int32, (1, 128), 1)
    lane_group = lax.div(lane, QB)

    inputs[0].wait()
    inputs[1].wait()
    slot = lax.broadcasted_iota(jnp.int32, (L, 128), 0)
    q32 = jnp.stack(
        [jnp.where(slot < qlen_ref[i], qraw[i].astype(F32), 0.0) for i in range(QB)], axis=0
    )
    qbuf[z] = jnp.swapaxes(q32, 0, 1).reshape(N, 128).astype(BF)


    inputs[4].wait()
    qa = lax.broadcasted_iota(jnp.int32, (QB, 128), 0)
    qb = lax.broadcasted_iota(jnp.int32, (QB, 128), 1)
    sq_wide = nn(sq_ref[...], (qa == lax.rem(qb, QB)).astype(BF))
    packed = jnp.zeros((8, 128), F32)
    for g in range(3):
        packed = jnp.where(lane_group == g, sq_wide[8 * g : 8 * g + 8], packed)
    sqx[c] = packed
    sp_wide = sp_ref[...].astype(F32)
    spt[k, z] = jnp.concatenate(
        [sp_wide[24 * u + 8 * g : 24 * u + 8 * g + 8] for g in range(3) for u in range(PR)], axis=0
    ).astype(BF)

    inputs[5].wait()
    wanted = jnp.zeros((1, 128), F32)
    within = lax.rem(lane, QB)
    for i in range(QB):
        wanted = jnp.where(within == i, pos_ref[i].astype(F32), wanted)
    wanted_ref[...] = wanted

    inputs[2].wait()
    inputs[3].wait()
    pslot = lax.broadcasted_iota(jnp.int32, (LP, 128), 0)
    p32 = []
    for i in range(8):
        rows = praw[i].astype(F32)
        p32.append(jnp.where(pslot < plen_ref[i], rows, rows[0:1]))
    xbuf[k] = jnp.swapaxes(jnp.stack(p32, axis=0), 0, 1).reshape(LP * 8, 128).astype(BF)

    def maxsim(tokens, zz):
        s = nt(tokens, qbuf[zz])
        m = jnp.max(s.reshape(-1, LP, 8, N), axis=1).reshape(-1, N)
        acc = m[:, 0:128]
        for t in range(1, N // 128):
            acc = acc + m[:, 128 * t : 128 * t + 128]
        return spread(acc)

    def teach(zz):
        tblk[zz] = maxsim(xbuf[...].reshape(2 * LP * 8, 128), zz).reshape(2, 8, 128)
        send(tblk.at[zz], town.at[z], many_send.at[12], many_recv.at[12], row=row_of(zz, k))

    tblk[z, k] = maxsim(xbuf[k], z)

    @pl.when(row_place + col_place > 0)
    def _():
        pl.semaphore_wait(barrier, row_place + col_place)

    for peer, later, back in edges:

        @pl.when(jnp.logical_not(later))
        def _(peer=peer, back=back):
            pl.semaphore_signal(near_sem.at[back], inc=1, device_id=peer, device_id_type=MESH)


    mine = pl.ds(pl.multiple_of(color * SL, SL), SL)
    mine_a = pl.ds(pl.multiple_of(color * SL, HALF), HALF)
    mine_b = pl.ds(pl.multiple_of(color * SL + HALF, HALF), HALF)

    half = Z // 2
    ways = (jnp.where(z < 2, 1, 0), jnp.where(z < 2, 0, 1))
    levels = [[(w, s) for w in ways] for s in range(1, half)] + [[(0, half)]]
    numbers = [[2 * n + w for w in range(len(level))] for n, level in enumerate(levels)]

    def block(way, s):
        return lax.rem(z + (2 * way - 1) * s + Z, Z)

    blocks = [(way, s) for level in levels for way, s in level]

    def z_step(way, s):
        b = block(way, s - 1)
        send(
            qbuf.at[b, mine], qbuf.at[b, mine], z_send.at[way, s - 1], z_recv.at[way, s - 1], row=row_of(z + 1 - 2 * way, k)
        )

    def z_got(way, s):
        got(qbuf.at[block(way, s), mine], z_recv.at[way, s - 1])

    def xy_regions():
        one = lax.rem(color + 3, 4) * SL
        two = lax.rem(color + 1, 4) * SL
        far = lax.rem(color + 2, 4) * SL
        return (
            pl.ds(pl.multiple_of(one, SL), SL),
            pl.ds(pl.multiple_of(two, SL), SL),
            pl.ds(pl.multiple_of(far, HALF), HALF),
            pl.ds(pl.multiple_of(far + HALF, HALF), HALF),
        )

    def xy_step(j):
        b = block(*blocks[j])
        beside = (col_of(x + 1, y), col_of(x - 1, y))
        above = (col_of(x, y + 1), col_of(x, y - 1))
        to = [jnp.where(k == 0, a, b) for a, b in zip(beside + above, above + beside)]
        for n, (part, peer) in enumerate(zip((mine, mine, mine_a, mine_b), to)):
            send(qbuf.at[b, part], qbuf.at[b, part], xy_send.at[n, j], xy_recv.at[n, j], col=peer)

    def xy_got(j):
        b = block(*blocks[j])
        for n, part in enumerate(xy_regions()):
            got(qbuf.at[b, part], xy_recv.at[n, j])

    def far_first(i, n):
        step = lax.div(i, 2)
        return n // 2 + jnp.where(lax.rem(i, 2) == 0, step, -step)

    def to_col(src_of, dst, n):
        def body(i, carry):
            peer = lax.rem(c + far_first(i, C), C)
            send(src_of(peer), dst, many_send.at[n], many_recv.at[n], col=peer)
            return carry

        lax.fori_loop(1, C, body, 0)

    def to_row(src_of, dst, n):
        def body(i, carry):
            peer = lax.rem(r + far_first(i, R), R)
            send(src_of(peer), dst, many_send.at[n], many_recv.at[n], row=peer)
            return carry

        lax.fori_loop(1, R, body, 0)

    def to_z(buf, n):
        def body(i, carry):
            send(buf.at[k, z], buf.at[k, z], many_send.at[n], many_recv.at[n], row=row_of(z + i, k))
            return carry

        lax.fori_loop(1, Z, body, 0)

    def z_to_sib(buf, n, m):
        got(buf.at[0, pl.ds(0, Z - 1)], many_recv.at[n])
        send(buf.at[k], buf.at[k], many_send.at[m], many_recv.at[m], row=row_of(z, 1 - k))

    lead = jnp.where(z == 0, 0, 1)
    for way in (lead, 1 - lead):

        @pl.when(jnp.where(way == 0, edges[1][1], edges[2][1]))
        def _(way=way):
            pl.semaphore_wait(near_sem.at[1 + way], 1)

        z_step(way, 1)
    edge(0)
    send(xbuf.at[k], xbuf.at[k], sib_send, sib_recv, row=row_of(z, 1 - k))
    greet(far_sem, (0, row_place), (0, col_place))

    p_index = c * PB + rows_p

    def onehot():
        return p_index.astype(F32) == wanted_ref[...]

    def student_scores():
        part = jnp.zeros((PB, 128), F32)
        order = [PR * (2 * zz + kk) + u for kk in range(2) for zz in range(Z) for u in range(PR)]
        rhs = jnp.concatenate([sqx[i] for i in order], axis=0).astype(BF)
        unit = lax.broadcasted_iota(jnp.int32, (PB, PB), 0) == lax.broadcasted_iota(jnp.int32, (PB, PB), 1)
        unit = unit.astype(BF)
        for g in range(3):
            wide = spt[:, :, 8 * PR * g : 8 * PR * (g + 1), :].reshape(2 * Z * 8 * PR, PB)
            back = nt(unit, wide).astype(BF)
            part = jnp.where(lane_group == g, nn(back, rhs), part)
        s = SCALE * spread(part)
        quarter = PB // GROUPS
        small = jnp.zeros((quarter, 128), F32)
        for g in range(GROUPS):
            small = jnp.where(lane_group == g, s[quarter * g : quarter * (g + 1)], small)
        top = jnp.max(s, axis=0, keepdims=True)
        mass = jnp.sum(jnp.exp(s - top), axis=0, keepdims=True)
        hit = jnp.sum(jnp.where(onehot(), s, 0.0), axis=0, keepdims=True)
        return s, small, jnp.where(lane_group == 0, top, jnp.where(lane_group == 1, mass, hit))

    def score_student():
        got(sqx.at[pl.ds(0, C - 1)], many_recv.at[0])
        got(spt.at[1 - k], many_recv.at[14])
        s, small, parts = student_scores()
        sbuf[...] = s
        zag[k, z] = small
        sst[c] = parts
        to_col(lambda peer: sst.at[c], sst.at[c], 3)
        to_z(zag, 6)
        to_row(lambda peer: sqx.at[pl.ds(PR * peer, PR)], sqr.at[r], 4)
        sqr[r] = sqx[pl.ds(PR * r, PR)]

    def only(v, g):
        return spread(jnp.where(lane_group == g, v, 0.0))

    def pack(dst, weights):
        hi, lo = split2(weights)
        table = spt[...].reshape(2 * Z * DR, PB)
        u = nn(jnp.concatenate([table, table], axis=1), jnp.concatenate([hi, lo], axis=0))
        for kk in range(2):
            for zz in range(Z):
                for uu in range(PR):
                    base = (kk * Z + zz) * DR + 8 * uu
                    piece = jnp.zeros((8, 128), F32)
                    for g in range(3):
                        at = base + 8 * PR * g
                        piece = jnp.where(lane_group == g, u[at : at + 8], piece)
                    dst[PR * (2 * zz + kk) + uu] = piece

    def softmax_parts(buf):
        rows = jnp.concatenate([buf[i] for i in range(C)], axis=0)
        tops = only(rows, 0)
        top = jnp.max(tops, axis=0, keepdims=True)
        weights = jnp.exp(tops - top)
        mass = only(jnp.sum(jnp.where(lane_group == 1, weights * rows, 0.0), axis=0, keepdims=True), 1)
        return top, mass, only(jnp.sum(rows, axis=0, keepdims=True), 2), weights

    def student_slopes():
        got(sst.at[pl.ds(0, C - 1)], many_recv.at[3])
        top, mass, hit, _ = softmax_parts(sst)
        zz_ = 2.0 * (jnp.exp(sbuf[...] - top) / mass) - jnp.where(onehot(), 1.0, 0.0)
        pack(upz, zz_)
        vbuf[c] = upz[c]
        to_col(lambda peer: upz.at[peer], vbuf.at[c], 5)
        sfin[r] = jnp.where(lane_group == 0, top, jnp.where(lane_group == 1, 1.0 / mass, wanted_ref[...]))
        to_row(lambda peer: sfin.at[r], sfin.at[r], 2)
        return top + jnp.log(mass), hit

    def owner(t, b):
        return 2 * (GROUPS * (t % (T // 2)) + b) + t // (T // 2)

    def row_vector(buf, t, g):
        tile = jnp.zeros((1, 128), F32)
        for b in range(GROUPS):
            v = buf[owner(t, b)]
            tile = jnp.where(lane_group == b, pltpu.roll(v, ((b - g) % GROUPS) * QB, 1) if b != g else v, tile)
        return tile

    def unpack_slopes():
        got(zag.at[1 - k], many_recv.at[7])
        got(sfin.at[pl.ds(0, R - 1)], many_recv.at[2])
        quarter = PB // GROUPS
        places = p_index.astype(F32)
        for t in range(T):
            for g in range(GROUPS):
                tile = jnp.zeros((quarter, 128), F32)
                for b in range(GROUPS):
                    rr = owner(t, b)
                    v = zag[rr % 2, rr // 2]
                    if b != g:
                        v = pltpu.roll(v, ((b - g) % GROUPS) * QB, 1)
                    tile = jnp.where(lane_group == b, v, tile)
                zfull[t, quarter * g : quarter * (g + 1)] = tile
            probs = jnp.exp(zfull[t] - row_vector(sfin, t, 0)) * row_vector(sfin, t, 1)
            zfull[t] = 2.0 * probs - jnp.where(places == row_vector(sfin, t, 2), 1.0, 0.0)

    def unpack_queries():
        got(sqr.at[pl.ds(0, R - 1)], many_recv.at[4])
        tiles = []
        for t in range(T):
            rows = []
            for u in range(PR):
                for g in range(3):
                    tile = jnp.zeros((8, 128), F32)
                    for b in range(GROUPS):
                        v = sqr[owner(t, b), u]
                        if b != g:
                            v = pltpu.roll(v, ((b - g) % GROUPS) * QB, 1)
                        tile = jnp.where(lane_group == b, v, tile)
                    rows.append(tile)
            tiles.append(jnp.concatenate(rows, axis=0).astype(BF))
        return tiles

    def turn(n, w):
        way, s = levels[n][w]
        z_got(way, s)
        if s < half - 1:
            z_step(way, s + 1)
        if n == half - 2:

            @pl.when(way == 0)
            def _():
                z_step(0, half)

        if n == 0 and w == 0:
            for e in (3, 4, 5, 6):
                edge(e)
        xy_step(numbers[n][w])

    turn(0, 0)
    turn(0, 1)
    got(xbuf.at[1 - k], sib_recv)
    tblk[z, 1 - k] = maxsim(xbuf[1 - k], z)
    town[z] = tblk[z]

    @pl.when(row_place + col_place < R + C - 2)
    def _():
        pl.semaphore_wait(far_sem, R - 1 - row_place + C - 1 - col_place)

    to_z(spt, 1)
    steps = [0, *range(2, len(blocks)), 1]
    for i, j in enumerate(steps):
        if i == 0:
            if half > 2:
                turn(1, 0)
            to_col(lambda peer: sqx.at[c], sqx.at[c], 0)
            if half > 2:
                turn(1, 1)
        if i in (1, 2) and half > 3:
            turn(2, i - 1)
        if i == max(1, len(steps) - 4):
            z_to_sib(spt, 1, 14)
        if i == max(1, len(steps) - 3):
            turn(half - 1, 0)
            score_student()
        xy_got(j)
        teach(block(*blocks[j]))

    for t in range(T // 2):
        tile = tblk[GROUPS * t]
        for b in range(1, GROUPS):
            tile = jnp.where(lane_group == b, tblk[GROUPS * t + b], tile)
        tag[k, z, t] = tile
    student_lse, hit = student_slopes()
    z_to_sib(zag, 6, 7)
    got(tblk.at[pl.ds(0, Z - 1)], many_recv.at[12])
    t_own = town[...].reshape(PB, 128)
    top = jnp.max(t_own, axis=0, keepdims=True)
    e = jnp.exp(t_own - top)
    mass = jnp.sum(e, axis=0, keepdims=True)
    cross = jnp.sum(e * (t_own - sbuf[...]), axis=0, keepdims=True)
    tst[c] = jnp.where(lane_group == 0, top, jnp.where(lane_group == 1, mass, cross))
    to_col(lambda peer: tst.at[c], tst.at[c], 13)
    pack(upt, e)
    ubuf[c] = upt[c]

    @pl.when(k == 0)
    def _():
        to_col(lambda peer: upt.at[peer], ubuf.at[c], 10)

    to_z(tag, 8)
    sq_tiles = unpack_queries()
    got(vbuf.at[pl.ds(0, C - 1)], many_recv.at[5])
    v_sum = functools.reduce(jnp.add, [vbuf[i] for i in range(C)])
    unpack_slopes()

    got(tst.at[pl.ds(0, C - 1)], many_recv.at[13])
    top, mass, _, weights = softmax_parts(tst)
    rows = jnp.concatenate([tst[i] for i in range(C)], axis=0)
    cross = only(jnp.sum(weights * rows, axis=0, keepdims=True), 2)
    inverse = 1.0 / mass
    per_query = cross * inverse - (top + jnp.log(mass)) + 2.0 * student_lse - hit
    fin[r] = jnp.where(lane_group == 0, top, jnp.where(lane_group == 1, inverse, per_query))
    to_row(lambda peer: fin.at[r], fin.at[r], 11)

    @pl.when(k == 1)
    def _():
        to_col(lambda peer: upt.at[peer], ubuf.at[c], 10)

    z_to_sib(tag, 8, 9)
    got(ubuf.at[pl.ds(0, C - 1)], many_recv.at[10])
    acc = jnp.zeros((8, 128), F32)
    for i in range(C):
        acc = acc + weights[i : i + 1] * ubuf[i]
    grads = (SCALE / total) * (v_sum - acc * inverse)
    for g in range(3):
        qg_ref[8 * g : 8 * g + 8, :] = (pltpu.roll(grads, 128 - QB * g, 1) if g else grads)[:, 0:QB]
    got(tag.at[1 - k], many_recv.at[9])

    got(fin.at[pl.ds(0, R - 1)], many_recv.at[11])
    grads = jnp.zeros((DR, PB), F32)
    per_query = jnp.zeros((1, 128), F32)
    for t in range(T):
        tops = row_vector(fin, t, 0)
        inverses = row_vector(fin, t, 1)
        for b in range(GROUPS):
            per_query = per_query + jnp.where(lane_group == 2, fin[owner(t, b)], 0.0)
        slopes = zfull[t] - jnp.exp(tag[t // (T // 2), :, t % (T // 2)].reshape(PB, 128) - tops) * inverses
        hi, lo = split2(slopes)
        grads = grads + nt(jnp.concatenate([sq_tiles[t]] * 2, axis=1), jnp.concatenate([hi, lo], axis=1))
    pg_ref[...] = grads * (SCALE / total)
    loss_ref[...] = jnp.zeros((1, 1), F32) + jnp.sum(per_query) / total

    for s in range(1, half + 1):
        left(qbuf.at[z, mine], z_send.at[0, s - 1])
        if s < half:
            left(qbuf.at[z, mine], z_send.at[1, s - 1])
    for j in range(len(blocks)):
        for n, part in enumerate((mine, mine, mine_a, mine_b)):
            left(qbuf.at[z, part], xy_send.at[n, j])
    left(xbuf.at[k], sib_send)
    for n, buf, count in ((0, sqx, C), (2, sfin, R), (13, tst, C), (3, sst, C), (5, upz, C), (10, upt, C), (4, sqr, R), (11, fin, R), (12, tblk, Z)):
        left(buf.at[pl.ds(0, count - 1)], many_send.at[n])
    for n, m, buf in ((1, 14, spt), (6, 7, zag), (8, 9, tag)):
        left(buf.at[0, pl.ds(0, Z - 1)], many_send.at[n])
        left(buf.at[0], many_send.at[m])


def hand_over(pg_ref, qg_ref, loss_ref, pg_out, qg_out, loss_out):
    pg_out[...] = pg_ref[...]
    qg_out[...] = qg_ref[...]
    loss_out[...] = loss_ref[...]


def shards(query_tokens, query_lengths, passage_tokens, passage_lengths, student_queries, student_passages, positives):
    R = lax.axis_size("row")
    C = lax.axis_size("col")
    Z = R // 2
    L = query_tokens.shape[1]
    LP = passage_tokens.shape[1]
    PB = 8 * R
    PR = C // R
    DR = student_passages.shape[1]
    T = R // GROUPS
    hops = Z - 1
    dma = pltpu.SemaphoreType.DMA
    vmem = pl.BlockSpec(memory_space=pltpu.VMEM)
    hbm = pl.BlockSpec(memory_space=pltpu.HBM)
    pg, qg, loss = pl.pallas_call(
        functools.partial(kernel, R, C),
        out_shape=(
            jax.ShapeDtypeStruct((DR, PB), F32),
            jax.ShapeDtypeStruct((24, QB), F32),
            jax.ShapeDtypeStruct((1, 1), F32),
        ),
        in_specs=[hbm] * 4 + [vmem] + [hbm] * 2,
        out_specs=(vmem, vmem, vmem),
        scratch_shapes=[
            pltpu.SMEM((QB,), jnp.int32),
            pltpu.SMEM((8,), jnp.int32),
            pltpu.SMEM((QB,), jnp.int32),
            pltpu.VMEM((1, 128), F32),
            pltpu.VMEM((DR, PB), BF),
            pltpu.VMEM((QB, L, 128), BF),
            pltpu.VMEM((8, LP, 128), BF),
            pltpu.VMEM((Z, QB * L, 128), BF),
            pltpu.VMEM((2, LP * 8, 128), BF),
            pltpu.VMEM((C, 8, 128), F32),
            pltpu.VMEM((2, Z, DR, PB), BF),
            pltpu.VMEM((C, 1, 128), F32),
            pltpu.VMEM((PB, 128), F32),
            pltpu.VMEM((C, 8, 128), F32),
            pltpu.VMEM((C, 8, 128), F32),
            pltpu.VMEM((2, Z, PB // GROUPS, 128), F32),
            pltpu.VMEM((T, PB, 128), F32),
            pltpu.VMEM((R, PR, 8, 128), F32),
            pltpu.VMEM((Z, 2, 8, 128), F32),
            pltpu.VMEM((Z, 2, 8, 128), F32),
            pltpu.VMEM((2, Z, T // 2, 2, 8, 128), F32),
            pltpu.VMEM((C, 8, 128), F32),
            pltpu.VMEM((C, 8, 128), F32),
            pltpu.VMEM((C, 1, 128), F32),
            pltpu.VMEM((R, 1, 128), F32),
            pltpu.VMEM((R, 1, 128), F32),
            dma((7,)),
            pltpu.SemaphoreType.REGULAR((7,)),
            pltpu.SemaphoreType.REGULAR,
            dma((2, Z // 2)),
            dma((2, Z // 2)),
            dma((4, hops)),
            dma((4, hops)),
            dma,
            dma,
            dma((15,)),
            dma((15,)),
        ],
        compiler_params=pltpu.CompilerParams(
            collective_id=0, has_side_effects=True, vmem_limit_bytes=64 * 1024 * 1024
        ),
        name="distill",
    )(query_tokens, query_lengths, passage_tokens, passage_lengths, student_queries.T, student_passages.T, positives)
    pg, qg, loss = pl.pallas_call(
        hand_over,
        out_shape=tuple(jax.ShapeDtypeStruct(a.shape, a.dtype) for a in (pg, qg, loss)),
        in_specs=[vmem] * 3,
        out_specs=(vmem, vmem, vmem),
        name="hand_over",
    )(pg, qg, loss)
    return qg.T, pg.T, loss.reshape(())


def solution(mesh):
    return jax.shard_map(
        shards,
        mesh=mesh,
        in_specs=(
            P("row", None, None),
            P("row"),
            P(("col", "row"), None, None),
            P(("col", "row")),
            P("row", "col"),
            P("col", "row"),
            P("row"),
        ),
        out_specs=(P("row", "col"), P("col", "row"), P()),
        check_vma=False,
    )
```
